32 devices in a mesh: groups: 2 (over y), band: 4 (over z), sub: 2 (over x), cfg: 2 (over core).
Axes of the slice: x: 2, y: 2, z: 4, core: 2. Of those that a mesh axis runs over, the one named last changes fastest.
Arguments:
- latents: float32 [32, 32, 256], P('groups', 'band', 'sub'), parts along dimension 0, may hold values from -6 to 6
- in_weight: bfloat16 [3, 3, 16, 320], replicated, may hold values from -0.5 to 0.5
- mid_weight: bfloat16 [3, 3, 320, 320], replicated, may hold values from -0.109375 to 0.109375
- out_weight: bfloat16 [3, 3, 16, 320], replicated, may hold values from -0.109375 to 0.109375
- norm_mean: float32 [2, 320], replicated, may hold values from -3 to 3
- norm_rstd: float32 [2, 320], replicated, may hold values from 0.5 to 2
- cond_embed: float32 [2, 640], P('cfg', 'groups'), parts along dimension 1, may hold values from -6 to 6
- time_embed: float32 [1000, 320], replicated, may hold values from -6 to 6
- time_index: int32 [2], replicated, may hold values from 0 to 999
- coef_index: int32 [2], replicated, may hold values from 0 to 999
- sampler_table: float32 [3, 1000], replicated, may hold values from -0.4 to 4, as said below
Outputs:
- denoised: float32 [32, 32, 256], P('groups', 'band', 'sub'), parts along dimension 0
The draws below stay inside these ranges and needn't reach their ends.
There are 2 independent parts, one for each index of `groups`. The reference program is written for one: setup_inputs(seed, part) draws one part's arguments, and reference() takes and returns one part's arrays. A program takes and returns all parts, laid end to end along the dimension named above; an argument that names none is the same for every part. Nothing has to cross between parts.
Inputs may be any that keep to these rules, and one draw needn't show every extreme that they name: `sampler_table`: column k holds one sampler step: row 0 scales the latent (0.8 to 1.2), row 1 scales the guided noise (-0.4 to -0.1), row 2 is the guidance scale (1.5 to 4.0).
All inputs are finite; a program needn't handle non-finite values.
Results may differ from the reference program's by a relative error of at most 0.013.
Values may be sent and summed in bfloat16 or wider, within the bound.
A program may use at most 64 MiB of HBM per device.

```python
import math
import jax
import jax.numpy as jnp
from jax import lax

CH = 16
FEAT = 320
TSTEPS = 1000
NCOEF = 1000
STEPS = 2
ROWS_DEV = 8
HEIGHT = 32
WIDTH = 256


def draw_sampler_table(key, part):
    spread = jax.random.uniform(key, (3, NCOEF), jnp.float32)
    low_end = jnp.array([[0.8], [-0.4], [1.5]], jnp.float32)
    high_end = jnp.array([[1.2], [-0.1], [4.0]], jnp.float32)
    return low_end + (high_end - low_end) * spread


def steps_of(key, shape, cuts, smallest, high):
    def one(dim, blocks):
        draws = jax.random.uniform(jax.random.fold_in(jax.random.fold_in(key, 6), dim), (blocks,), jnp.float32, smallest / len(cuts), high / len(cuts))
        return jnp.repeat(jnp.exp(draws), shape[dim] // blocks).reshape((-1,) + (1,) * (len(shape) - dim - 1))

    factor_of = one(*cuts[0])
    for cut in cuts[1:]:
        factor_of = factor_of * one(*cut)
    return factor_of


def scatter_about(key, shape, deviation, reach, split=(), held_as=jnp.bfloat16):
    entries = jax.random.normal(key, shape, jnp.float32) * deviation
    if len(split) > 0:
        entries = steps_of(key, shape, split, -0.22, 0.18) * entries
    return jnp.clip(entries, min=-reach, max=reach).astype(held_as)


def setup_inputs(seed: int = 0, part: int = 0) -> dict:
    key_of = jax.random.split(jax.random.key(seed), 12)
    part_keys = jax.random.split(jax.random.fold_in(key_of[11], part), 12)
    latents = scatter_about(part_keys[0], (CH, HEIGHT, WIDTH), 1.0, 6.0, ((1, 4), (2, 2)), jnp.float32)
    in_weight = scatter_about(key_of[1], (3, 3, CH, FEAT), (9 * CH) ** -0.5, 0.5)
    mid_weight = scatter_about(key_of[2], (3, 3, FEAT, FEAT), (9 * FEAT) ** -0.5, 0.109375)
    out_weight = scatter_about(key_of[3], (3, 3, CH, FEAT), (9 * FEAT) ** -0.5, 0.109375)
    norm_mean = scatter_about(key_of[4], (2, FEAT), 0.5, 3.0, (), jnp.float32)
    norm_rstd = jnp.clip(jnp.exp(jax.random.uniform(key_of[5], (2, FEAT), jnp.float32, math.log(0.5), math.log(2.0))), 0.5, 2.0)
    cond_embed = scatter_about(part_keys[6], (2, FEAT), 1.0, 6.0, ((0, 2),), jnp.float32)
    time_embed = scatter_about(key_of[7], (TSTEPS, FEAT), 1.0, 6.0, (), jnp.float32)
    time_index = jax.random.randint(key_of[8], (STEPS,), 0, TSTEPS).astype(jnp.int32)
    coef_index = jax.random.randint(key_of[9], (STEPS,), 0, NCOEF).astype(jnp.int32)
    sampler_table = draw_sampler_table(jax.random.fold_in(key_of[11], 71), part)
    return dict(latents=latents, in_weight=in_weight, mid_weight=mid_weight, out_weight=out_weight, norm_mean=norm_mean, norm_rstd=norm_rstd, cond_embed=cond_embed, time_embed=time_embed, time_index=time_index, coef_index=coef_index, sampler_table=sampler_table)


def conv_valid(source, kernel, pattern):
    out_rows = source.shape[1] - 2
    out_cols = source.shape[2] - 2
    total = None
    for tap_row in range(3):
        for tap_col in range(3):
            window = source[:, tap_row:tap_row + out_rows, tap_col:tap_col + out_cols].astype(jnp.float32)
            product = jnp.einsum(pattern, kernel[tap_row, tap_col].astype(jnp.float32), window, precision=lax.Precision.HIGHEST)
            total = product if total is None else total + product
    return total


def activate(field, centre, spread):
    return jax.nn.silu((field - centre[:, None, None]) * spread[:, None, None]).astype(jnp.bfloat16)


def noise_region(source, inside, kernels, offset):
    in_weight, mid_weight, out_weight, norm_mean, norm_rstd = kernels
    first_map = conv_valid(source * inside, in_weight, "co,chw->ohw") + offset[:, None, None]
    lifted = activate(first_map, norm_mean[0], norm_rstd[0]) * inside[1:-1, 1:-1]
    second = first_map[:, 1:-1, 1:-1] + conv_valid(lifted, mid_weight, "oc,chw->ohw")
    lowered = activate(second, norm_mean[1], norm_rstd[1]) * inside[2:-2, 2:-2]
    return conv_valid(lowered, out_weight, "oc,chw->ohw")


def noise_field(source, offset, kernels):
    height = source.shape[1]
    width = source.shape[2]
    padded = jnp.pad(source, ((0, 0), (3, 3), (3, 3)))
    row_place = jnp.arange(height + 6, dtype=jnp.int32) - 3
    col_place = jnp.arange(width + 6, dtype=jnp.int32) - 3
    col_inside = (col_place >= 0) & (col_place < width)
    block_count = height // ROWS_DEV

    def one_block(block_id):
        start = (block_id * ROWS_DEV).astype(jnp.int32)
        piece = lax.dynamic_slice_in_dim(padded, start, ROWS_DEV + 6, 1)
        rows_here = lax.dynamic_slice_in_dim(row_place, start, ROWS_DEV + 6, 0)
        row_inside = (rows_here >= 0) & (rows_here < height)
        inside = (row_inside[:, None] & col_inside[None, :]).astype(jnp.bfloat16)
        return noise_region(piece, inside, kernels, offset)

    pieces = lax.map(one_block, jnp.arange(block_count, dtype=jnp.int32))
    return jnp.transpose(pieces, (1, 0, 2, 3)).reshape(source.shape[0], height, width)


def reference(latents, in_weight, mid_weight, out_weight, norm_mean, norm_rstd, cond_embed, time_embed, time_index, coef_index, sampler_table):
    kernels = (in_weight, mid_weight, out_weight, norm_mean, norm_rstd)
    current = latents
    for sample_step in range(STEPS):
        time_row = lax.dynamic_index_in_dim(time_embed, time_index[sample_step], 0, keepdims=False)
        sampler_col = lax.dynamic_index_in_dim(sampler_table, coef_index[sample_step], 1, keepdims=False)
        source = current.astype(jnp.bfloat16)
        plain_noise = noise_field(source, time_row + cond_embed[0], kernels)
        steered_noise = noise_field(source, time_row + cond_embed[1], kernels)
        guided = plain_noise + sampler_col[2] * (steered_noise - plain_noise)
        current = sampler_col[0] * current + sampler_col[1] * guided
    return current
```

```python
import functools

import jax
import jax.numpy as jnp
from jax import lax
from jax.experimental import pallas as pl
from jax.experimental.pallas import tpu as pltpu
from jax.sharding import PartitionSpec as P

LANES = 128
TILE = 256


def up(value, unit):
    return -(-value // unit) * unit


def turned(field, by, stride):
    return pltpu.roll(field, by % stride, 0)


def spread_taps(ref, base, field, stride, chans):
    rows = field.shape[0] // stride
    for tap in range(3):
        parts = [
            turned(field[k * stride : (k + 1) * stride], 1 - tap, stride) if tap != 1 else field[k * stride : (k + 1) * stride]
            for k in range(rows)
        ]
        for k in range(rows):
            ref[pl.ds(pl.multiple_of(base + k * stride, 16), stride), tap * chans : (tap + 1) * chans] = parts[k].astype(jnp.bfloat16)


def section_kernel(
    geom, coef_ref, lat_ref, win_ref, wide_ref, thin_ref, wout_ref, vec_ref, out_ref,
    state, taps, first, lift, thin, low, mixed,
):
    steps, height, cols, stride, margin, feat, chans = geom
    wide = feat // TILE * TILE
    rest = feat - wide
    row_home = lax.axis_index("band") * height
    image_rows = lax.axis_size("band") * height
    image_cols = lax.axis_size("sub") * lax.axis_size("cfg") * cols
    col_home = (lax.axis_index("sub") * lax.axis_size("cfg") + lax.axis_index("cfg")) * cols - margin

    def inside(row, lanes):
        place = lax.broadcasted_iota(jnp.int32, (stride, lanes), 0) + col_home
        image_row = row_home + row
        limit = jnp.where((image_row >= 0) & (image_row < image_rows), image_cols, 0)
        return (place >= 0) & (place < limit)

    def at(row, count=1):
        return pl.ds(pl.multiple_of(row * stride, 16), count * stride)

    copies = LANES // chans
    tall = jnp.concatenate([lat_ref[...]] * copies, axis=0)
    state[...] = jnp.transpose(tall)
    group = lax.broadcasted_iota(jnp.int32, (stride, LANES), 1) // chans

    for step in range(steps):
        edge = margin - 3 * step
        rows = height + 2 * edge
        firsts = rows - 2
        seconds = rows - 4
        last = step == steps - 1
        scale1 = vec_ref[0:1, :]
        scale2 = vec_ref[1:2, :]
        base = 2 + 4 * step
        shift1 = [vec_ref[base + q : base + q + 1, :] for q in range(2)]
        shift2 = [vec_ref[base + 2 + q : base + 3 + q, :] for q in range(2)]

        def lay(row, carry):
            field = state[at(row), :]
            before = turned(field, 1, stride)
            after = turned(field, -1, stride)
            mixed_row = jnp.where(group % 3 == 0, before, jnp.where(group % 3 == 1, field, after))
            mixed[at(row), 0:LANES] = mixed_row
            mixed[at(row), LANES : 2 * LANES] = after
            return carry

        lax.fori_loop(0, rows, lay, 0)

        def gather(row, carry):
            one = mixed[at(row), 0:LANES]
            two = mixed[at(row + 1), 0:LANES]
            three = mixed[at(row + 2), 0:LANES]
            body = jnp.where(group < 3, one, jnp.where(group < 6, two, three))
            taps[at(row), 0:LANES] = body.astype(jnp.bfloat16)
            taps[at(row), LANES : LANES + chans] = mixed[at(row + 2), LANES : LANES + chans].astype(jnp.bfloat16)
            return carry

        lax.fori_loop(0, firsts, gather, 0)

        def lead(pair, carry):
            row = pair * 2
            field = jnp.dot(taps[at(row, 2), :], win_ref[...], preferred_element_type=jnp.float32)
            first[at(row, 2), :] = field
            for k in range(2):
                keep = inside(row + k + 1 - edge, feat)
                for q in range(2):
                    half = field[k * stride : (k + 1) * stride] * scale1 + shift1[q]
                    value = jnp.where(keep, half + half * jnp.tanh(half), 0.0)
                    spread_taps(lift.at[q], (row + k) * stride, value, stride, feat)
            return carry

        lax.fori_loop(0, firsts // 2, lead, 0)

        chunk = 6 if firsts % 6 == 0 else 2

        def narrow(k, carry):
            for q in range(2):
                thin[q, at(k * chunk, chunk), :] = jnp.dot(
                    lift[q, at(k * chunk, chunk), :], thin_ref[...], preferred_element_type=jnp.float32
                )
            return carry

        lax.fori_loop(0, firsts // chunk, narrow, 0)

        count = 4 if seconds % 4 == 0 else (5 if seconds % 5 == 0 else 2)
        gain = coef_ref[step, 2]

        def middle(k, carry):
            row = k * count
            lowered = None
            for q in range(2):
                total = first[at(row + 1, count), 0:wide]
                for tap in range(3):
                    total = total + jnp.dot(
                        lift[q, at(row + tap, count), :], wide_ref[tap], preferred_element_type=jnp.float32
                    )
                tail = first[at(row + 1, count), wide:feat]
                for tap in range(3):
                    tail = tail + thin[q, at(row + tap, count), tap * rest : (tap + 1) * rest]
                both = []
                for field, part in ((total, slice(0, wide)), (tail, slice(wide, feat))):
                    half = field * scale2[:, part] + shift2[q][:, part]
                    both.append(half + half * jnp.tanh(half))
                if q == 0:
                    lowered = both
                else:
                    lowered = [a + gain * (b - a) for a, b in zip(lowered, both)]
            for part_values, start in zip(lowered, (0, wide)):
                width = part_values.shape[1]
                for m in range(count):
                    keep = inside(row + m + 2 - edge, width)
                    value = jnp.where(keep, part_values[m * stride : (m + 1) * stride], 0.0)
                    for tap in range(3):
                        moved = value if tap == 1 else turned(value, 1 - tap, stride)
                        low[at(row + m), tap * feat + start : tap * feat + start + width] = moved.astype(jnp.bfloat16)
            return carry

        lax.fori_loop(0, seconds // count, middle, 0)

        def close(k, carry):
            mixed2 = jnp.dot(low[at(k * 2, 2), :], wout_ref[...], preferred_element_type=jnp.float32)
            noise[at(k * 2, 2), :] = mixed2
            return carry

        noise = mixed
        lax.fori_loop(0, seconds // 2, close, 0)

        def finish(row, carry):
            total = noise[at(row), 0:LANES]
            total = total + noise[at(row + 1), LANES : 2 * LANES]
            total = total + noise[at(row + 2), 2 * LANES : 3 * LANES]
            value = coef_ref[step, 0] * state[at(row + 3), :] + coef_ref[step, 1] * total
            if not last:
                value = jnp.where(inside(row + 3 - edge, LANES), value, 0.0)
            state[at(row), :] = value
            return carry

        lax.fori_loop(0, rows - 6, finish, 0)

    out_ref[...] = jnp.transpose(state[0 : up(height * stride, LANES), :])[0:chans, :]


def shards(
    latents, in_weight, mid_weight, out_weight, norm_mean, norm_rstd,
    cond_embed, time_embed, time_index, coef_index, sampler_table,
):
    chans, height, full_cols = latents.shape
    feat = in_weight.shape[3]
    steps = time_index.shape[0]
    margin = 3 * steps
    parts = lax.axis_size("cfg")
    subs = lax.axis_size("sub")
    bands = lax.axis_size("band")
    cols = full_cols // parts
    stride = up(cols + 2 * margin, 16)
    rows = height + 2 * margin
    wide = feat // TILE * TILE
    rest = feat - wide
    mine = lax.axis_index("cfg")

    sent = latents.astype(jnp.bfloat16)
    above = lax.ppermute(sent[:, -margin:], "band", [(i, i + 1) for i in range(bands - 1)])
    below = lax.ppermute(sent[:, :margin], "band", [(i + 1, i) for i in range(bands - 1)])
    tall = jnp.concatenate([above.astype(jnp.float32), latents, below.astype(jnp.float32)], axis=1)
    edge = jnp.where(mine == 0, tall[:, :, -margin:], tall[:, :, :margin]).astype(jnp.bfloat16)
    route = [(s * parts, (s + 1) * parts) for s in range(subs - 1)]
    route += [((s + 1) * parts + 1, s * parts + 1) for s in range(subs - 1)]
    beside = lax.ppermute(edge, ("sub", "cfg"), route).astype(jnp.float32)
    window = jnp.where(
        mine == 0,
        jnp.concatenate([beside, tall[:, :, : cols + margin]], axis=2),
        jnp.concatenate([tall[:, :, full_cols - cols - margin :], beside], axis=2),
    )
    window = jnp.pad(window, ((0, 0), (0, 0), (0, stride - cols - 2 * margin)))
    pixels = rows * stride
    held = up(pixels, LANES)
    window = jnp.pad(window.reshape(chans, pixels), ((0, 0), (0, held - pixels)))

    other = lax.ppermute(cond_embed, "cfg", [(0, 1), (1, 0)])
    plain = jnp.where(mine == 0, cond_embed, other)[0]
    steered = jnp.where(mine == 0, other, cond_embed)[0]
    half = 0.5 * norm_rstd
    lines = [half[0], half[1]]
    coefs = []
    for step in range(steps):
        time_row = lax.dynamic_index_in_dim(time_embed, time_index[step], 0, keepdims=False)
        coefs.append(lax.dynamic_index_in_dim(sampler_table, coef_index[step], 1, keepdims=False))
        for layer in range(2):
            for cond in (plain, steered):
                lines.append((time_row + cond - norm_mean[layer]) * half[layer])
    vecs = jnp.stack(lines)
    vecs = jnp.pad(vecs, ((0, up(vecs.shape[0], 8) - vecs.shape[0]), (0, 0)))
    coefs = jnp.stack(coefs)

    win = in_weight.reshape(9 * chans, feat)
    wmid = jnp.transpose(mid_weight, (0, 1, 3, 2)).reshape(3, 3 * feat, feat)
    wwide = wmid[:, :, :wide]
    wthin = jnp.transpose(wmid[:, :, wide:], (1, 0, 2)).reshape(3 * feat, 3 * rest)
    copies = LANES // chans
    wout = jnp.transpose(out_weight, (1, 3, 0, 2)).reshape(3 * feat, 3, 1, chans)
    wout = jnp.broadcast_to(wout, (3 * feat, 3, copies, chans)).reshape(3 * feat, 3 * LANES)

    geom = (steps, height, cols, stride, margin, feat, chans)
    whole = pl.BlockSpec(memory_space=pltpu.VMEM)
    firsts = (rows - 2) * stride
    seconds = (rows - 4) * stride
    out = pl.pallas_call(
        functools.partial(section_kernel, geom),
        out_shape=jax.ShapeDtypeStruct((chans, up(height * stride, LANES)), jnp.float32),
        in_specs=[pl.BlockSpec(memory_space=pltpu.SMEM)] + [whole] * 6,
        out_specs=whole,
        scratch_shapes=[
            pltpu.VMEM((held, LANES), jnp.float32),
            pltpu.VMEM((firsts, 9 * chans), jnp.bfloat16),
            pltpu.VMEM((firsts, feat), jnp.float32),
            pltpu.VMEM((2, firsts, 3 * feat), jnp.bfloat16),
            pltpu.VMEM((2, firsts, 3 * rest), jnp.float32),
            pltpu.VMEM((seconds, 3 * feat), jnp.bfloat16),
            pltpu.VMEM((rows * stride, 3 * LANES), jnp.float32),
        ],
        compiler_params=pltpu.CompilerParams(vmem_limit_bytes=48 * 1024 * 1024),
    )(coefs, window, win, wwide, wthin, wout, vecs)
    out = out[:, : height * stride].reshape(chans, height, stride)[:, :, margin : margin + cols]
    far = lax.ppermute(out, "cfg", [(0, 1), (1, 0)])
    return jnp.where(
        mine == 0, jnp.concatenate([out, far], axis=2), jnp.concatenate([far, out], axis=2)
    )


def solution(mesh):
    return jax.shard_map(
        shards,
        mesh=mesh,
        in_specs=(P("groups", "band", "sub"), P(), P(), P(), P(), P(), P("cfg", "groups"), P(), P(), P(), P()),
        out_specs=P("groups", "band", "sub"),
        check_vma=False,
    )
```

```python
import functools

import jax
import jax.numpy as jnp
from jax import lax
from jax.experimental import pallas as pl
from jax.experimental.pallas import tpu as pltpu
from jax.sharding import PartitionSpec as P

LANES = 128
TILE = 256
MESH = pl.DeviceIdType.MESH


def up(value, unit):
    return -(-value // unit) * unit


def turned(field, tap):
    return field if tap == 1 else pltpu.roll(field, (1 - tap) % field.shape[0], 0)


def section_kernel(
    geom, time_at, coef_at, table, lat_ref, win_ref, mid_hbm, wout_ref, mean_ref, rstd_ref, cond_ref, time_hbm, out_ref,
    state, taps, first, lift0, lift1, thin0, thin1, low, mixed,
    mid_ref, time_ref, wide_ref, narrow_ref, last_ref, vec_ref,
    row_send, row_recv, col_send, col_recv, cond_recv, half_send, half_recv,
    local_sem, send_sem, recv_sem,
):
    steps, height, full_cols, cols, stride, margin, feat, chans = geom
    wide = feat // TILE * TILE
    rest = feat - wide
    depth = 3 * wide + up(3 * rest, TILE)
    side = (stride - cols) // 2
    lifts = (lift0, lift1)
    thins = (thin0, thin1)
    band, sub, mine = (lax.axis_index(name) for name in ("band", "sub", "cfg"))
    bands, subs, parts = (lax.axis_size(name) for name in ("band", "sub", "cfg"))
    row_home = band * height
    image_rows = bands * height
    image_cols = subs * parts * cols
    col_home = (sub * parts + mine) * cols - side
    first_core = mine == 0

    def inside(row, lanes):
        place = lax.broadcasted_iota(jnp.int32, (stride, lanes), 0) + col_home
        image_row = row_home + row
        limit = jnp.where((image_row >= 0) & (image_row < image_rows), image_cols, 0)
        return (place >= 0) & (place < limit)

    def at(row, count=1):
        return pl.ds(pl.multiple_of(row * stride, 16), count * stride)

    ahead = jnp.where(first_core, sub + 1, sub - 1)
    behind = jnp.where(first_core, sub - 1, sub + 1)
    goes = (ahead >= 0) & (ahead < subs)
    comes = (behind >= 0) & (behind < subs)
    has_up = band > 0
    has_down = band < bands - 1
    partner = {"cfg": 1 - mine}

    mid_copy = pltpu.make_async_copy(mid_hbm, mid_ref, local_sem.at[0])
    time_copy = pltpu.make_async_copy(time_hbm, time_ref, local_sem.at[1])
    mid_copy.start()
    time_copy.start()

    barrier = pltpu.get_barrier_semaphore()

    def greet(when, device):
        @pl.when(when)
        def _():
            pl.semaphore_signal(barrier, inc=1, device_id=device, device_id_type=MESH)

    greet(has_up, {"band": band - 1})
    greet(has_down, {"band": band + 1})
    greet(comes, {"sub": behind})
    greet(comes & has_up, {"band": band - 1, "sub": behind})
    greet(comes & has_down, {"band": band + 1, "sub": behind})
    pl.semaphore_signal(barrier, inc=1, device_id=partner, device_id_type=MESH)

    copies = LANES // chans
    for y in range(height):
        row_send[y * chans : (y + 1) * chans, :] = lat_ref[:, y, :].astype(jnp.bfloat16)

    def stand(block):
        return jnp.transpose(jnp.concatenate([block] * copies, axis=0))

    bodies = [stand(lat_ref[:, y, :]) for y in range(height)]
    for y in range(0, height, 2):
        pair = [
            jnp.where(first_core, bodies[y + k][full_cols - side :], bodies[y + k][:side]) for k in range(2)
        ]
        col_send[y * side : (y + 2) * side, :] = jnp.concatenate(pair, axis=0).astype(jnp.bfloat16)

    def count(flag):
        return flag.astype(jnp.int32)

    pl.semaphore_wait(
        barrier,
        1 + count(has_up) + count(has_down) + count(goes) + count(goes & has_up) + count(goes & has_down),
    )

    rows = height + 2 * margin
    row_part = margin * chans
    col_part = margin * side

    def remote(k, source, target, device):
        return pltpu.make_async_remote_copy(
            src_ref=source, dst_ref=target, send_sem=send_sem.at[k], recv_sem=recv_sem.at[k],
            device_id=device, device_id_type=MESH,
        )

    row_all = height * chans
    col_all = height * side
    sends = [
        (has_down, has_up, remote(0, row_send.at[row_all - row_part : row_all], row_recv.at[0:row_part], {"band": band + 1})),
        (has_up, has_down, remote(1, row_send.at[0:row_part], row_recv.at[row_part : 2 * row_part], {"band": band - 1})),
        (goes, comes, remote(2, col_send, col_recv.at[col_part : col_part + col_all], {"sub": ahead})),
        (goes & has_down, comes & has_up, remote(3, col_send.at[col_all - col_part : col_all], col_recv.at[0:col_part], {"band": band + 1, "sub": ahead})),
        (goes & has_up, comes & has_down, remote(4, col_send.at[0:col_part], col_recv.at[col_part + col_all : 2 * col_part + col_all], {"band": band - 1, "sub": ahead})),
    ]
    for go, come, copy in sends:
        pl.when(go)(copy.start)
    cond_copy = remote(5, cond_ref, cond_recv, partner)
    cond_copy.start()

    mid_copy.wait()
    for i in range(3):
        for j in range(3):
            turned_mid = jnp.transpose(mid_ref[i, j].astype(jnp.float32)).astype(jnp.bfloat16)
            base = i * depth
            wide_ref[base + j * wide : base + (j + 1) * wide, :] = turned_mid[:wide, :wide]
            narrow_ref[j * wide : (j + 1) * wide, i * rest : (i + 1) * rest] = turned_mid[:wide, wide:]
            spot = 3 * wide + j * rest
            wide_ref[base + spot : base + spot + rest, :] = turned_mid[wide:, :wide]
            narrow_ref[spot : spot + rest, i * rest : (i + 1) * rest] = turned_mid[wide:, wide:]
            small = wout_ref[i, j].astype(jnp.float32)
            tall = jnp.transpose(jnp.concatenate([small] * copies, axis=0)).astype(jnp.bfloat16)
            last_ref[j * wide : (j + 1) * wide, i * LANES : (i + 1) * LANES] = tall[:wide]
            last_ref[spot : spot + rest, i * LANES : (i + 1) * LANES] = tall[wide:]
        spare = 3 * wide + 3 * rest
        wide_ref[i * depth + spare : (i + 1) * depth, :] = jnp.zeros((depth - spare, wide), jnp.bfloat16)
    narrow_ref[spare:, :] = jnp.zeros((depth - spare, 3 * rest), jnp.bfloat16)
    last_ref[spare:, :] = jnp.zeros((depth - spare, 3 * LANES), jnp.bfloat16)

    cond_copy.wait()
    time_copy.wait()
    plain = jnp.where(first_core, cond_ref[...], cond_recv[...])
    steered = jnp.where(first_core, cond_recv[...], cond_ref[...])
    half_rstd = 0.5 * rstd_ref[...]
    vec_ref[0:2, :] = half_rstd
    for step in range(steps):
        time_row = time_ref[pl.ds(time_at[step], 1), :]
        for layer in range(2):
            for q, cond in enumerate((plain, steered)):
                line = 2 + 4 * step + 2 * layer + q
                vec_ref[line : line + 1, :] = (time_row + cond - mean_ref[layer : layer + 1, :]) * half_rstd[layer : layer + 1, :]

    def wait_for(copy):
        def both():
            copy.wait_recv()

        return both

    for go, come, copy in sends:
        pl.when(go)(copy.wait_send)
        pl.when(come)(wait_for(copy))

    for row in range(rows):
        if margin <= row < margin + height:
            body = bodies[row - margin]
        else:
            spot = row if row < margin else row - height
            body = stand(row_recv[spot * chans : (spot + 1) * chans, :].astype(jnp.float32))
        pair = col_recv[row // 2 * 2 * side : (row // 2 * 2 + 2) * side, :].astype(jnp.float32)
        border = pair[row % 2 * side : (row % 2 + 1) * side]
        field = jnp.where(
            first_core,
            jnp.concatenate([border, body[: cols + side]], axis=0),
            jnp.concatenate([body[full_cols - cols - side :], border], axis=0),
        )
        state[row * stride : (row + 1) * stride, :] = jnp.where(inside(row - margin, LANES), field, 0.0)

    group = lax.broadcasted_iota(jnp.int32, (stride, LANES), 1) // chans

    def silu_of(half):
        return half + half * jnp.tanh(half)

    def spread(ref, row, big, small):
        for tap in range(3):
            ref[at(row), tap * wide : (tap + 1) * wide] = turned(big, tap).astype(jnp.bfloat16)
        ends = [turned(small, tap) for tap in range(3)]
        ends.append(jnp.zeros((stride, depth - 3 * wide - 3 * rest), jnp.float32))
        ref[at(row), 3 * wide : depth] = jnp.concatenate(ends, axis=1).astype(jnp.bfloat16)

    for step in range(steps):
        edge = margin - 3 * step
        now_rows = height + 2 * edge
        firsts = now_rows - 2
        seconds = now_rows - 4
        is_last = step == steps - 1
        base = 2 + 4 * step

        def lay(row, carry):
            field = state[at(row), :]
            before = turned(field, 0)
            after = turned(field, 2)
            mixed[at(row), 0:LANES] = jnp.where(group % 3 == 0, before, jnp.where(group % 3 == 1, field, after))
            mixed[at(row), LANES : 2 * LANES] = after
            return carry

        lax.fori_loop(0, now_rows, lay, 0)

        chunk = 6 if firsts % 6 == 0 else 2

        def lead(k, carry):
            row = k * chunk
            for m in range(chunk):
                one = mixed[at(row + m), 0:LANES]
                two = mixed[at(row + m + 1), 0:LANES]
                three = mixed[at(row + m + 2), 0:LANES]
                body = jnp.where(group < 3, one, jnp.where(group < 6, two, three))
                taps[at(m), 0:LANES] = body.astype(jnp.bfloat16)
                taps[at(m), LANES : LANES + chans] = mixed[at(row + m + 2), LANES : LANES + chans].astype(jnp.bfloat16)
            field = jnp.dot(taps[...][: chunk * stride], win_ref[...], preferred_element_type=jnp.float32)
            first[at(row, chunk), :] = field
            for q in range(2):
                shift = vec_ref[base + q : base + q + 1, :]
                for m in range(chunk):
                    here = field[m * stride : (m + 1) * stride]
                    keep = inside(row + m + 1 - edge, wide)
                    parts = []
                    for part in (slice(0, wide), slice(wide, feat)):
                        value = silu_of(here[:, part] * vec_ref[0:1, part] + shift[:, part])
                        parts.append(jnp.where(keep[:, : value.shape[1]], value, 0.0))
                    spread(lifts[q], row + m, *parts)
                thins[q][at(row, chunk), :] = jnp.dot(
                    lifts[q][at(row, chunk), :], narrow_ref[...], preferred_element_type=jnp.float32
                )
            return carry

        lax.fori_loop(0, firsts // chunk, lead, 0)

        count2 = 4 if seconds % 4 == 0 else (5 if seconds % 5 == 0 else 2)
        gain = table[2, coef_at[step]]

        def middle(k, carry):
            row = k * count2
            found = []
            for q in range(2):
                window = jnp.concatenate([lifts[q][at(row + tap, count2), :] for tap in range(3)], axis=1)
                total = first[at(row + 1, count2), 0:wide] + jnp.dot(
                    window, wide_ref[...], preferred_element_type=jnp.float32
                )
                tail = first[at(row + 1, count2), wide:feat]
                for tap in range(3):
                    tail = tail + thins[q][at(row + tap, count2), tap * rest : (tap + 1) * rest]
                shift = vec_ref[base + 2 + q : base + 3 + q, :]
                found.append(
                    [
                        silu_of(field * vec_ref[1:2, part] + shift[:, part])
                        for field, part in ((total, slice(0, wide)), (tail, slice(wide, feat)))
                    ]
                )
            lowered = [a + gain * (b - a) for a, b in zip(*found)]
            for m in range(count2):
                keep = inside(row + m + 2 - edge, wide)
                spread(
                    low,
                    row + m,
                    *[
                        jnp.where(keep[:, : part.shape[1]], part[m * stride : (m + 1) * stride], 0.0)
                        for part in lowered
                    ],
                )
            mixed[at(row, count2), :] = jnp.dot(low[at(row, count2), :], last_ref[...], preferred_element_type=jnp.float32)
            return carry

        lax.fori_loop(0, seconds // count2, middle, 0)

        keeps = table[0, coef_at[step]]
        adds = table[1, coef_at[step]]

        def finish(row, carry):
            total = mixed[at(row), 0:LANES] + mixed[at(row + 1), LANES : 2 * LANES]
            total = total + mixed[at(row + 2), 2 * LANES : 3 * LANES]
            value = keeps * state[at(row + 3), :] + adds * total
            if not is_last:
                value = jnp.where(inside(row + 3 - edge, LANES), value, 0.0)
            state[at(row), :] = value
            return carry

        lax.fori_loop(0, now_rows - 6, finish, 0)

    group = lax.broadcasted_iota(jnp.int32, (cols, LANES), 1) // chans
    packed = state[side : side + cols, :]
    for y in range(1, height):
        packed = jnp.where(group == y, state[y * stride + side : y * stride + side + cols, :], packed)
    half_send[...] = packed
    swap = remote(6, half_send, half_recv, partner)
    swap.start()
    swap.wait()
    other = half_recv[...]
    joined = jnp.concatenate(
        [jnp.where(first_core, packed, other), jnp.where(first_core, other, packed)], axis=0
    )
    flat = jnp.transpose(joined)
    for y in range(height):
        out_ref[y] = flat[y * chans : (y + 1) * chans]


def shards(
    latents, in_weight, mid_weight, out_weight, norm_mean, norm_rstd,
    cond_embed, time_embed, time_index, coef_index, sampler_table,
):
    chans, height, full_cols = latents.shape
    feat = in_weight.shape[3]
    steps = time_index.shape[0]
    margin = 3 * steps
    cols = full_cols // lax.axis_size("cfg")
    stride = up(cols + 2 * margin, 16)
    side = (stride - cols) // 2
    rows = height + 2 * margin
    wide = feat // TILE * TILE
    rest = feat - wide
    depth = 3 * wide + up(3 * rest, TILE)
    win = in_weight.reshape(9 * chans, feat)
    geom = (steps, height, full_cols, cols, stride, margin, feat, chans)
    whole = pl.BlockSpec(memory_space=pltpu.VMEM)
    scalars = pl.BlockSpec(memory_space=pltpu.SMEM)
    far = pl.BlockSpec(memory_space=pl.ANY)
    firsts = (rows - 2) * stride
    seconds = (rows - 4) * stride
    out = pl.pallas_call(
        functools.partial(section_kernel, geom),
        out_shape=jax.ShapeDtypeStruct((height, chans, full_cols), jnp.float32),
        in_specs=[scalars] * 3 + [whole, whole, far, whole, whole, whole, whole, far],
        out_specs=whole,
        scratch_shapes=[
            pltpu.VMEM((rows * stride, LANES), jnp.float32),
            pltpu.VMEM((6 * stride, 9 * chans), jnp.bfloat16),
            pltpu.VMEM((firsts, feat), jnp.float32),
            pltpu.VMEM((firsts, depth), jnp.bfloat16),
            pltpu.VMEM((firsts, depth), jnp.bfloat16),
            pltpu.VMEM((firsts, 3 * rest), jnp.float32),
            pltpu.VMEM((firsts, 3 * rest), jnp.float32),
            pltpu.VMEM((seconds, depth), jnp.bfloat16),
            pltpu.VMEM((rows * stride, 3 * LANES), jnp.float32),
            pltpu.VMEM(mid_weight.shape, mid_weight.dtype),
            pltpu.VMEM(time_embed.shape, time_embed.dtype),
            pltpu.VMEM((3 * depth, wide), jnp.bfloat16),
            pltpu.VMEM((depth, 3 * rest), jnp.bfloat16),
            pltpu.VMEM((depth, 3 * LANES), jnp.bfloat16),
            pltpu.VMEM((up(2 + 4 * steps, 8), feat), jnp.float32),
            pltpu.VMEM((height * chans, full_cols), jnp.bfloat16),
            pltpu.VMEM((2 * margin * chans, full_cols), jnp.bfloat16),
            pltpu.VMEM((height * side, LANES), jnp.bfloat16),
            pltpu.VMEM((rows * side, LANES), jnp.bfloat16),
            pltpu.VMEM(cond_embed.shape, jnp.float32),
            pltpu.VMEM((cols, LANES), jnp.float32),
            pltpu.VMEM((cols, LANES), jnp.float32),
            pltpu.SemaphoreType.DMA((2,)),
            pltpu.SemaphoreType.DMA((7,)),
            pltpu.SemaphoreType.DMA((7,)),
        ],
        compiler_params=pltpu.CompilerParams(
            vmem_limit_bytes=48 * 1024 * 1024, collective_id=0, has_side_effects=True
        ),
    )(
        time_index, coef_index, sampler_table, latents, win, mid_weight, out_weight,
        norm_mean, norm_rstd, cond_embed, time_embed,
    )
    return jnp.transpose(out, (1, 0, 2))


def solution(mesh):
    return jax.shard_map(
        shards,
        mesh=mesh,
        in_specs=(P("groups", "band", "sub"), P(), P(), P(), P(), P(), P("cfg", "groups"), P(), P(), P(), P()),
        out_specs=P("groups", "band", "sub"),
        check_vma=False,
    )
```

```python
import functools

import jax
import jax.numpy as jnp
from jax import lax
from jax.experimental import pallas as pl
from jax.experimental.pallas import tpu as pltpu
from jax.sharding import PartitionSpec as P

LANES = 128
TILE = 256
MESH = pl.DeviceIdType.MESH


def up(value, unit):
    return -(-value // unit) * unit


def turned(field, tap):
    return field if tap == 1 else pltpu.roll(field, (1 - tap) % field.shape[0], 0)


def section_kernel(
    geom, time_at, coef_at, table, lat_ref, win_ref, mid_hbm, wout_ref, mean_ref, rstd_ref, cond_ref, time_hbm, out_ref,
    state, taps, first, lift0, lift1, thin0, thin1, low, mixed,
    mid_ref, time_ref, wide_ref, narrow_ref, last_ref, vec_ref,
    row_send, row_recv, col_send, col_recv, cond_recv, half_send, half_recv, outside_ref,
    local_sem, send_sem, recv_sem,
):
    steps, height, full_cols, cols, stride, margin, feat, chans = geom
    wide = feat // TILE * TILE
    rest = feat - wide
    depth = 3 * wide + up(3 * rest, TILE)
    side = (stride - cols) // 2
    lifts = (lift0, lift1)
    thins = (thin0, thin1)
    band, sub, mine = (lax.axis_index(name) for name in ("band", "sub", "cfg"))
    bands, subs, parts = (lax.axis_size(name) for name in ("band", "sub", "cfg"))
    row_home = band * height
    image_rows = bands * height
    image_cols = subs * parts * cols
    col_home = (sub * parts + mine) * cols - side
    first_core = mine == 0

    place = lax.broadcasted_iota(jnp.int32, (stride, wide), 0) + col_home
    outside_ref[...] = jnp.where((place >= 0) & (place < image_cols), 0, 1)

    def inside(row, lanes):
        image_row = row_home + row
        limit = jnp.where((image_row >= 0) & (image_row < image_rows), 1, 0)
        return outside_ref[:, :lanes] < limit

    def at(row, count=1):
        return pl.ds(pl.multiple_of(row * stride, 16), count * stride)

    ahead = jnp.where(first_core, sub + 1, sub - 1)
    behind = jnp.where(first_core, sub - 1, sub + 1)
    goes = (ahead >= 0) & (ahead < subs)
    comes = (behind >= 0) & (behind < subs)
    has_up = band > 0
    has_down = band < bands - 1
    partner = {"cfg": 1 - mine}

    mid_copy = pltpu.make_async_copy(mid_hbm, mid_ref, local_sem.at[0])
    time_copy = pltpu.make_async_copy(time_hbm, time_ref, local_sem.at[1])
    mid_copy.start()
    time_copy.start()

    barrier = pltpu.get_barrier_semaphore()

    def greet(when, device):
        @pl.when(when)
        def _():
            pl.semaphore_signal(barrier, inc=1, device_id=device, device_id_type=MESH)

    greet(has_up, {"band": band - 1})
    greet(has_down, {"band": band + 1})
    greet(comes, {"sub": behind})
    greet(comes & has_up, {"band": band - 1, "sub": behind})
    greet(comes & has_down, {"band": band + 1, "sub": behind})
    pl.semaphore_signal(barrier, inc=1, device_id=partner, device_id_type=MESH)

    copies = LANES // chans
    for y in range(height):
        row_send[y * chans : (y + 1) * chans, :] = lat_ref[:, y, :].astype(jnp.bfloat16)

    def stand(block):
        return jnp.transpose(jnp.concatenate([block] * copies, axis=0))

    bodies = [stand(lat_ref[:, y, :]) for y in range(height)]
    for y in range(0, height, 2):
        pair = [
            jnp.where(first_core, bodies[y + k][full_cols - side :], bodies[y + k][:side]) for k in range(2)
        ]
        col_send[y * side : (y + 2) * side, :] = jnp.concatenate(pair, axis=0).astype(jnp.bfloat16)

    def count(flag):
        return flag.astype(jnp.int32)

    pl.semaphore_wait(
        barrier,
        1 + count(has_up) + count(has_down) + count(goes) + count(goes & has_up) + count(goes & has_down),
    )

    rows = height + 2 * margin
    row_part = margin * chans
    col_part = margin * side

    def remote(k, source, target, device):
        return pltpu.make_async_remote_copy(
            src_ref=source, dst_ref=target, send_sem=send_sem.at[k], recv_sem=recv_sem.at[k],
            device_id=device, device_id_type=MESH,
        )

    row_all = height * chans
    col_all = height * side
    sends = [
        (has_down, has_up, remote(0, row_send.at[row_all - row_part : row_all], row_recv.at[0:row_part], {"band": band + 1})),
        (has_up, has_down, remote(1, row_send.at[0:row_part], row_recv.at[row_part : 2 * row_part], {"band": band - 1})),
        (goes, comes, remote(2, col_send, col_recv.at[col_part : col_part + col_all], {"sub": ahead})),
        (goes & has_down, comes & has_up, remote(3, col_send.at[col_all - col_part : col_all], col_recv.at[0:col_part], {"band": band + 1, "sub": ahead})),
        (goes & has_up, comes & has_down, remote(4, col_send.at[0:col_part], col_recv.at[col_part + col_all : 2 * col_part + col_all], {"band": band - 1, "sub": ahead})),
    ]
    for go, come, copy in sends:
        pl.when(go)(copy.start)
    cond_copy = remote(5, cond_ref, cond_recv, partner)
    cond_copy.start()

    mid_copy.wait()
    for i in range(3):
        for j in range(3):
            turned_mid = jnp.transpose(mid_ref[i, j])
            base = i * depth
            wide_ref[base + j * wide : base + (j + 1) * wide, :] = turned_mid[:wide, :wide]
            narrow_ref[j * wide : (j + 1) * wide, i * rest : (i + 1) * rest] = turned_mid[:wide, wide:]
            spot = 3 * wide + j * rest
            wide_ref[base + spot : base + spot + rest, :] = turned_mid[wide:, :wide]
            narrow_ref[spot : spot + rest, i * rest : (i + 1) * rest] = turned_mid[wide:, wide:]
            small = wout_ref[i, j].astype(jnp.float32)
            tall = jnp.transpose(jnp.concatenate([small] * copies, axis=0)).astype(jnp.bfloat16)
            span = slice(i * LANES // 2, (i + 1) * LANES // 2) if i < 2 else slice(LANES, 2 * LANES)
            tall = tall[:, : span.stop - span.start]
            last_ref[j * wide : (j + 1) * wide, span] = tall[:wide]
            last_ref[spot : spot + rest, span] = tall[wide:]
        spare = 3 * wide + 3 * rest
        wide_ref[i * depth + spare : (i + 1) * depth, :] = jnp.zeros((depth - spare, wide), jnp.bfloat16)
    narrow_ref[spare:, :] = jnp.zeros((depth - spare, 3 * rest), jnp.bfloat16)
    last_ref[spare:, :] = jnp.zeros((depth - spare, 2 * LANES), jnp.bfloat16)

    cond_copy.wait()
    time_copy.wait()
    plain = jnp.where(first_core, cond_ref[...], cond_recv[...])
    steered = jnp.where(first_core, cond_recv[...], cond_ref[...])
    half_rstd = 0.5 * rstd_ref[...]
    vec_ref[0:2, :] = half_rstd
    moments = lax.broadcasted_iota(jnp.int32, time_ref.shape, 1)
    for step in range(steps):
        column = jnp.sum(jnp.where(moments == time_at[step], time_ref[...], 0.0), axis=1, keepdims=True)
        time_row = jnp.transpose(jnp.broadcast_to(column, (feat, LANES)))[0:1]
        for layer in range(2):
            for q, cond in enumerate((plain, steered)):
                line = 2 + 4 * step + 2 * layer + q
                vec_ref[line : line + 1, :] = (time_row + cond - mean_ref[layer : layer + 1, :]) * half_rstd[layer : layer + 1, :]

    def wait_for(copy):
        def both():
            copy.wait_recv()

        return both

    for go, come, copy in sends:
        pl.when(go)(copy.wait_send)
        pl.when(come)(wait_for(copy))

    for row in range(rows):
        if margin <= row < margin + height:
            body = bodies[row - margin]
        else:
            spot = row if row < margin else row - height
            body = stand(row_recv[spot * chans : (spot + 1) * chans, :].astype(jnp.float32))
        pair = col_recv[row // 2 * 2 * side : (row // 2 * 2 + 2) * side, :].astype(jnp.float32)
        border = pair[row % 2 * side : (row % 2 + 1) * side]
        field = jnp.where(
            first_core,
            jnp.concatenate([border, body[: cols + side]], axis=0),
            jnp.concatenate([body[full_cols - cols - side :], border], axis=0),
        )
        state[row * stride : (row + 1) * stride, :] = jnp.where(inside(row - margin, LANES), field, 0.0)

    group = lax.broadcasted_iota(jnp.int32, (stride, LANES), 1) // chans

    def silu_of(half):
        return half + half * jnp.tanh(half)

    def spread(ref, row, big, small):
        for tap in range(3):
            ref[at(row), tap * wide : (tap + 1) * wide] = turned(big, tap).astype(jnp.bfloat16)
        ends = [turned(small, tap) for tap in range(3)]
        ends.append(jnp.zeros((stride, depth - 3 * wide - 3 * rest), jnp.float32))
        ref[at(row), 3 * wide : depth] = jnp.concatenate(ends, axis=1).astype(jnp.bfloat16)

    for step in range(steps):
        edge = margin - 3 * step
        now_rows = height + 2 * edge
        firsts = now_rows - 2
        seconds = now_rows - 4
        is_last = step == steps - 1
        base = 2 + 4 * step

        def lay(row, carry):
            field = state[at(row), :]
            before = turned(field, 0)
            after = turned(field, 2)
            mixed[at(row), 0:LANES] = jnp.where(group % 3 == 0, before, jnp.where(group % 3 == 1, field, after))
            mixed[at(row), LANES : 2 * LANES] = after
            return carry

        lax.fori_loop(0, now_rows, lay, 0)

        chunk = 6 if firsts % 6 == 0 else 2

        def lead(k, carry):
            row = k * chunk
            for m in range(chunk):
                one = mixed[at(row + m), 0:LANES]
                two = mixed[at(row + m + 1), 0:LANES]
                three = mixed[at(row + m + 2), 0:LANES]
                body = jnp.where(group < 3, one, jnp.where(group < 6, two, three))
                taps[at(m), 0:LANES] = body.astype(jnp.bfloat16)
                taps[at(m), LANES : LANES + chans] = mixed[at(row + m + 2), LANES : LANES + chans].astype(jnp.bfloat16)
            field = jnp.dot(taps[...][: chunk * stride], win_ref[...], preferred_element_type=jnp.float32)
            first[at(row, chunk), :] = field
            for q in range(2):
                shift = vec_ref[base + q : base + q + 1, :]
                for m in range(chunk):
                    here = field[m * stride : (m + 1) * stride]
                    keep = inside(row + m + 1 - edge, wide)
                    parts = []
                    for part in (slice(0, wide), slice(wide, feat)):
                        value = silu_of(here[:, part] * vec_ref[0:1, part] + shift[:, part])
                        parts.append(jnp.where(keep[:, : value.shape[1]], value, 0.0))
                    spread(lifts[q], row + m, *parts)
                thins[q][at(row, chunk), :] = jnp.dot(
                    lifts[q][at(row, chunk), :], narrow_ref[...], preferred_element_type=jnp.float32
                )
            return carry

        lax.fori_loop(0, firsts // chunk, lead, 0)

        count2 = 8 if seconds % 8 == 0 else (10 if seconds % 10 == 0 else 2)
        gain = table[2, coef_at[step]]

        def middle(k, carry):
            row = k * count2
            found = []
            for q in range(2):
                window = jnp.concatenate([lifts[q][at(row + tap, count2), :] for tap in range(3)], axis=1)
                total = first[at(row + 1, count2), 0:wide] + jnp.dot(
                    window, wide_ref[...], preferred_element_type=jnp.float32
                )
                tail = first[at(row + 1, count2), wide:feat]
                for tap in range(3):
                    tail = tail + thins[q][at(row + tap, count2), tap * rest : (tap + 1) * rest]
                shift = vec_ref[base + 2 + q : base + 3 + q, :]
                found.append(
                    [
                        silu_of(field * vec_ref[1:2, part] + shift[:, part])
                        for field, part in ((total, slice(0, wide)), (tail, slice(wide, feat)))
                    ]
                )
            lowered = [a + gain * (b - a) for a, b in zip(*found)]
            for m in range(count2):
                keep = inside(row + m + 2 - edge, wide)
                spread(
                    low,
                    row + m,
                    *[
                        jnp.where(keep[:, : part.shape[1]], part[m * stride : (m + 1) * stride], 0.0)
                        for part in lowered
                    ],
                )
            mixed[at(row, count2), :] = jnp.dot(low[at(row, count2), :], last_ref[...], preferred_element_type=jnp.float32)
            return carry

        lax.fori_loop(0, seconds // count2, middle, 0)

        keeps = table[0, coef_at[step]]
        adds = table[1, coef_at[step]]

        def finish(row, carry):
            total = jnp.where(group < LANES // 2 // chans, mixed[at(row), 0:LANES], mixed[at(row + 1), 0:LANES])
            total = total + pltpu.roll(total, LANES // 2, 1) + mixed[at(row + 2), LANES : 2 * LANES]
            value = keeps * state[at(row + 3), :] + adds * total
            if not is_last:
                value = jnp.where(inside(row + 3 - edge, LANES), value, 0.0)
            state[at(row), :] = value
            return carry

        lax.fori_loop(0, now_rows - 6, finish, 0)

    group = lax.broadcasted_iota(jnp.int32, (cols, LANES), 1) // chans
    packed = state[side : side + cols, :]
    for y in range(1, height):
        packed = jnp.where(group == y, state[y * stride + side : y * stride + side + cols, :], packed)
    half_send[...] = packed
    swap = remote(6, half_send, half_recv, partner)
    swap.start()
    swap.wait()
    other = half_recv[...]
    joined = jnp.concatenate(
        [jnp.where(first_core, packed, other), jnp.where(first_core, other, packed)], axis=0
    )
    flat = jnp.transpose(joined)
    for y in range(height):
        out_ref[y] = flat[y * chans : (y + 1) * chans]


def shards(
    latents, in_weight, mid_weight, out_weight, norm_mean, norm_rstd,
    cond_embed, time_embed, time_index, coef_index, sampler_table,
):
    chans, height, full_cols = latents.shape
    feat = in_weight.shape[3]
    steps = time_index.shape[0]
    margin = 3 * steps
    cols = full_cols // lax.axis_size("cfg")
    stride = up(cols + 2 * margin, 16)
    side = (stride - cols) // 2
    rows = height + 2 * margin
    wide = feat // TILE * TILE
    rest = feat - wide
    depth = 3 * wide + up(3 * rest, TILE)
    win = in_weight.reshape(9 * chans, feat)
    geom = (steps, height, full_cols, cols, stride, margin, feat, chans)
    whole = pl.BlockSpec(memory_space=pltpu.VMEM)
    scalars = pl.BlockSpec(memory_space=pltpu.SMEM)
    far = pl.BlockSpec(memory_space=pl.ANY)
    firsts = (rows - 2) * stride
    seconds = (rows - 4) * stride
    out = pl.pallas_call(
        functools.partial(section_kernel, geom),
        out_shape=jax.ShapeDtypeStruct((height, chans, full_cols), jnp.float32),
        in_specs=[scalars] * 3 + [whole, whole, far, whole, whole, whole, whole, far],
        out_specs=whole,
        scratch_shapes=[
            pltpu.VMEM((rows * stride, LANES), jnp.float32),
            pltpu.VMEM((6 * stride, 9 * chans), jnp.bfloat16),
            pltpu.VMEM((firsts, feat), jnp.float32),
            pltpu.VMEM((firsts, depth), jnp.bfloat16),
            pltpu.VMEM((firsts, depth), jnp.bfloat16),
            pltpu.VMEM((firsts, 3 * rest), jnp.float32),
            pltpu.VMEM((firsts, 3 * rest), jnp.float32),
            pltpu.VMEM((seconds, depth), jnp.bfloat16),
            pltpu.VMEM((rows * stride, 2 * LANES), jnp.float32),
            pltpu.VMEM(mid_weight.shape, mid_weight.dtype),
            pltpu.VMEM(time_embed.shape[::-1], time_embed.dtype),
            pltpu.VMEM((3 * depth, wide), jnp.bfloat16),
            pltpu.VMEM((depth, 3 * rest), jnp.bfloat16),
            pltpu.VMEM((depth, 2 * LANES), jnp.bfloat16),
            pltpu.VMEM((up(2 + 4 * steps, 8), feat), jnp.float32),
            pltpu.VMEM((height * chans, full_cols), jnp.bfloat16),
            pltpu.VMEM((2 * margin * chans, full_cols), jnp.bfloat16),
            pltpu.VMEM((height * side, LANES), jnp.bfloat16),
            pltpu.VMEM((rows * side, LANES), jnp.bfloat16),
            pltpu.VMEM(cond_embed.shape, jnp.float32),
            pltpu.VMEM((cols, LANES), jnp.float32),
            pltpu.VMEM((cols, LANES), jnp.float32),
            pltpu.VMEM((stride, wide), jnp.int32),
            pltpu.SemaphoreType.DMA((2,)),
            pltpu.SemaphoreType.DMA((7,)),
            pltpu.SemaphoreType.DMA((7,)),
        ],
        compiler_params=pltpu.CompilerParams(
            vmem_limit_bytes=60 * 1024 * 1024, collective_id=0, has_side_effects=True
        ),
    )(
        time_index, coef_index, sampler_table, latents, win, mid_weight, out_weight,
        norm_mean, norm_rstd, cond_embed, time_embed.T,
    )
    return jnp.transpose(out, (1, 0, 2))


def solution(mesh):
    return jax.shard_map(
        shards,
        mesh=mesh,
        in_specs=(P("groups", "band", "sub"), P(), P(), P(), P(), P(), P("cfg", "groups"), P(), P(), P(), P()),
        out_specs=P("groups", "band", "sub"),
        check_vma=False,
    )
```

```python
import functools

import jax
import jax.numpy as jnp
from jax import lax
from jax.experimental import pallas as pl
from jax.experimental.pallas import tpu as pltpu
from jax.sharding import PartitionSpec as P

LANES = 128
TILE = 256
MESH = pl.DeviceIdType.MESH


def up(value, unit):
    return -(-value // unit) * unit


def turned(field, tap):
    return field if tap == 1 else pltpu.roll(field, (1 - tap) % field.shape[0], 0)


def section_kernel(
    geom, time_at, coef_at, table, lat_ref, win_ref, mid_hbm, wout_ref, mean_ref, rstd_ref, cond_ref, time_hbm, out_ref,
    state, taps, first, lift0, lift1, thin0, thin1, low, mixed,
    mid_ref, time_ref, kernel_ref, last_ref, vec_ref,
    row_send, row_recv, col_send, col_recv, cond_recv, half_send, half_recv, outside_ref,
    local_sem, send_sem, recv_sem,
):
    steps, height, full_cols, cols, stride, margin, feat, chans = geom
    wide = feat // TILE * TILE
    rest = feat - wide
    depth = 3 * wide + up(3 * rest, TILE)
    side = (stride - cols) // 2
    lifts = (lift0, lift1)
    thins = (thin0, thin1)
    band, sub, mine = (lax.axis_index(name) for name in ("band", "sub", "cfg"))
    bands, subs, parts = (lax.axis_size(name) for name in ("band", "sub", "cfg"))
    row_home = band * height
    image_rows = bands * height
    image_cols = subs * parts * cols
    col_home = (sub * parts + mine) * cols - side
    first_core = mine == 0

    place = lax.broadcasted_iota(jnp.int32, (stride, wide), 0) + col_home
    outside_ref[...] = jnp.where((place >= 0) & (place < image_cols), 0, 1)

    def inside(row, lanes):
        image_row = row_home + row
        limit = jnp.where((image_row >= 0) & (image_row < image_rows), 1, 0)
        return outside_ref[:, :lanes] < limit

    def at(row, count=1):
        return pl.ds(pl.multiple_of(row * stride, 16), count * stride)

    ahead = jnp.where(first_core, sub + 1, sub - 1)
    behind = jnp.where(first_core, sub - 1, sub + 1)
    goes = (ahead >= 0) & (ahead < subs)
    comes = (behind >= 0) & (behind < subs)
    has_up = band > 0
    has_down = band < bands - 1
    partner = {"cfg": 1 - mine}

    mid_copy = pltpu.make_async_copy(mid_hbm, mid_ref, local_sem.at[0])
    time_copy = pltpu.make_async_copy(time_hbm, time_ref, local_sem.at[1])
    mid_copy.start()
    time_copy.start()

    barrier = pltpu.get_barrier_semaphore()

    def greet(when, device):
        @pl.when(when)
        def _():
            pl.semaphore_signal(barrier, inc=1, device_id=device, device_id_type=MESH)

    greet(has_up, {"band": band - 1})
    greet(has_down, {"band": band + 1})
    greet(comes, {"sub": behind})
    greet(comes & has_up, {"band": band - 1, "sub": behind})
    greet(comes & has_down, {"band": band + 1, "sub": behind})
    pl.semaphore_signal(barrier, inc=1, device_id=partner, device_id_type=MESH)

    copies = LANES // chans
    for y in range(height):
        row_send[y * chans : (y + 1) * chans, :] = lat_ref[:, y, :].astype(jnp.bfloat16)

    def stand(block):
        return jnp.transpose(jnp.concatenate([block] * copies, axis=0))

    bodies = [stand(lat_ref[:, y, :]) for y in range(height)]
    for y in range(0, height, 2):
        pair = [
            jnp.where(first_core, bodies[y + k][full_cols - side :], bodies[y + k][:side]) for k in range(2)
        ]
        col_send[y * side : (y + 2) * side, :] = jnp.concatenate(pair, axis=0).astype(jnp.bfloat16)

    def count(flag):
        return flag.astype(jnp.int32)

    pl.semaphore_wait(
        barrier,
        1 + count(has_up) + count(has_down) + count(goes) + count(goes & has_up) + count(goes & has_down),
    )

    rows = height + 2 * margin
    row_part = margin * chans
    col_part = margin * side

    def remote(k, source, target, device):
        return pltpu.make_async_remote_copy(
            src_ref=source, dst_ref=target, send_sem=send_sem.at[k], recv_sem=recv_sem.at[k],
            device_id=device, device_id_type=MESH,
        )

    row_all = height * chans
    col_all = height * side
    sends = [
        (has_down, has_up, remote(0, row_send.at[row_all - row_part : row_all], row_recv.at[0:row_part], {"band": band + 1})),
        (has_up, has_down, remote(1, row_send.at[0:row_part], row_recv.at[row_part : 2 * row_part], {"band": band - 1})),
        (goes, comes, remote(2, col_send, col_recv.at[col_part : col_part + col_all], {"sub": ahead})),
        (goes & has_down, comes & has_up, remote(3, col_send.at[col_all - col_part : col_all], col_recv.at[0:col_part], {"band": band + 1, "sub": ahead})),
        (goes & has_up, comes & has_down, remote(4, col_send.at[0:col_part], col_recv.at[col_part + col_all : 2 * col_part + col_all], {"band": band - 1, "sub": ahead})),
    ]
    for go, come, copy in sends:
        pl.when(go)(copy.start)
    cond_copy = remote(5, cond_ref, cond_recv, partner)
    cond_copy.start()

    mid_copy.wait()
    for i in range(3):
        for j in range(3):
            turned_mid = jnp.transpose(mid_ref[i, j])
            spot = 3 * wide + j * rest
            broad = slice(i * wide, (i + 1) * wide)
            slim = slice(3 * wide + i * rest, 3 * wide + (i + 1) * rest)
            kernel_ref[j * wide : (j + 1) * wide, broad] = turned_mid[:wide, :wide]
            kernel_ref[j * wide : (j + 1) * wide, slim] = turned_mid[:wide, wide:]
            kernel_ref[spot : spot + rest, broad] = turned_mid[wide:, :wide]
            kernel_ref[spot : spot + rest, slim] = turned_mid[wide:, wide:]
            small = wout_ref[i, j].astype(jnp.float32)
            tall = jnp.transpose(jnp.concatenate([small] * copies, axis=0)).astype(jnp.bfloat16)
            span = slice(i * LANES // 2, (i + 1) * LANES // 2) if i < 2 else slice(LANES, 2 * LANES)
            tall = tall[:, : span.stop - span.start]
            last_ref[j * wide : (j + 1) * wide, span] = tall[:wide]
            last_ref[spot : spot + rest, span] = tall[wide:]
    spare = 3 * feat
    kernel_ref[spare:, :] = jnp.zeros((depth - spare, 3 * feat), jnp.bfloat16)
    last_ref[spare:, :] = jnp.zeros((depth - spare, 2 * LANES), jnp.bfloat16)

    cond_copy.wait()
    time_copy.wait()
    plain = jnp.where(first_core, cond_ref[...], cond_recv[...])
    steered = jnp.where(first_core, cond_recv[...], cond_ref[...])
    half_rstd = 0.5 * rstd_ref[...]
    vec_ref[0:2, :] = half_rstd
    moments = lax.broadcasted_iota(jnp.int32, time_ref.shape, 1)
    for step in range(steps):
        column = jnp.sum(jnp.where(moments == time_at[step], time_ref[...], 0.0), axis=1, keepdims=True)
        time_row = jnp.transpose(jnp.broadcast_to(column, (feat, LANES)))[0:1]
        for layer in range(2):
            for q, cond in enumerate((plain, steered)):
                line = 2 + 4 * step + 2 * layer + q
                vec_ref[line : line + 1, :] = (time_row + cond - mean_ref[layer : layer + 1, :]) * half_rstd[layer : layer + 1, :]

    def wait_for(copy):
        def both():
            copy.wait_recv()

        return both

    for go, come, copy in sends:
        pl.when(go)(copy.wait_send)
        pl.when(come)(wait_for(copy))

    for row in range(rows):
        if margin <= row < margin + height:
            body = bodies[row - margin]
        else:
            spot = row if row < margin else row - height
            body = stand(row_recv[spot * chans : (spot + 1) * chans, :].astype(jnp.float32))
        pair = col_recv[row // 2 * 2 * side : (row // 2 * 2 + 2) * side, :].astype(jnp.float32)
        border = pair[row % 2 * side : (row % 2 + 1) * side]
        field = jnp.where(
            first_core,
            jnp.concatenate([border, body[: cols + side]], axis=0),
            jnp.concatenate([body[full_cols - cols - side :], border], axis=0),
        )
        state[row * stride : (row + 1) * stride, :] = jnp.where(inside(row - margin, LANES), field, 0.0)

    group = lax.broadcasted_iota(jnp.int32, (stride, LANES), 1) // chans

    def silu_of(half):
        return half + half * jnp.tanh(half)

    def spread(ref, row, big, small):
        for tap in range(3):
            ref[at(row), tap * wide : (tap + 1) * wide] = turned(big, tap).astype(jnp.bfloat16)
        ends = [turned(small, tap) for tap in range(3)]
        ends.append(jnp.zeros((stride, depth - 3 * wide - 3 * rest), jnp.float32))
        ref[at(row), 3 * wide : depth] = jnp.concatenate(ends, axis=1).astype(jnp.bfloat16)

    for step in range(steps):
        edge = margin - 3 * step
        now_rows = height + 2 * edge
        firsts = now_rows - 2
        seconds = now_rows - 4
        is_last = step == steps - 1
        base = 2 + 4 * step

        def lay(row, carry):
            field = state[at(row), :]
            before = turned(field, 0)
            after = turned(field, 2)
            mixed[at(row), 0:LANES] = jnp.where(group % 3 == 0, before, jnp.where(group % 3 == 1, field, after))
            mixed[at(row), LANES : 2 * LANES] = after
            return carry

        lax.fori_loop(0, now_rows, lay, 0)

        chunk = 6 if firsts % 6 == 0 else 2

        def lead(k, carry):
            row = k * chunk
            for m in range(chunk):
                one = mixed[at(row + m), 0:LANES]
                two = mixed[at(row + m + 1), 0:LANES]
                three = mixed[at(row + m + 2), 0:LANES]
                body = jnp.where(group < 3, one, jnp.where(group < 6, two, three))
                taps[at(m), 0:LANES] = body.astype(jnp.bfloat16)
                taps[at(m), LANES : LANES + chans] = mixed[at(row + m + 2), LANES : LANES + chans].astype(jnp.bfloat16)
            field = jnp.dot(taps[...][: chunk * stride], win_ref[...], preferred_element_type=jnp.float32)
            first[at(row, chunk), :] = field
            for q in range(2):
                shift = vec_ref[base + q : base + q + 1, :]
                for m in range(chunk):
                    here = field[m * stride : (m + 1) * stride]
                    keep = inside(row + m + 1 - edge, wide)
                    parts = []
                    for part in (slice(0, wide), slice(wide, feat)):
                        value = silu_of(here[:, part] * vec_ref[0:1, part] + shift[:, part])
                        parts.append(jnp.where(keep[:, : value.shape[1]], value, 0.0))
                    spread(lifts[q], row + m, *parts)
                thins[q][at(row, chunk), :] = jnp.dot(
                    lifts[q][at(row, chunk), :], kernel_ref[...], preferred_element_type=jnp.float32
                )
            return carry

        lax.fori_loop(0, firsts // chunk, lead, 0)

        count2 = 4 if seconds % 4 == 0 else (5 if seconds % 5 == 0 else 2)
        gain = table[2, coef_at[step]]

        def middle(k, carry):
            row = k * count2
            found = []
            for q in range(2):
                total = first[at(row + 1, count2), 0:wide]
                tail = first[at(row + 1, count2), wide:feat]
                for tap in range(3):
                    total = total + thins[q][at(row + tap, count2), tap * wide : (tap + 1) * wide]
                    spot = 3 * wide + tap * rest
                    tail = tail + thins[q][at(row + tap, count2), spot : spot + rest]
                shift = vec_ref[base + 2 + q : base + 3 + q, :]
                found.append(
                    [
                        silu_of(field * vec_ref[1:2, part] + shift[:, part])
                        for field, part in ((total, slice(0, wide)), (tail, slice(wide, feat)))
                    ]
                )
            lowered = [a + gain * (b - a) for a, b in zip(*found)]
            for m in range(count2):
                keep = inside(row + m + 2 - edge, wide)
                spread(
                    low,
                    row + m,
                    *[
                        jnp.where(keep[:, : part.shape[1]], part[m * stride : (m + 1) * stride], 0.0)
                        for part in lowered
                    ],
                )
            mixed[at(row, count2), :] = jnp.dot(low[at(row, count2), :], last_ref[...], preferred_element_type=jnp.float32)
            return carry

        lax.fori_loop(0, seconds // count2, middle, 0)

        keeps = table[0, coef_at[step]]
        adds = table[1, coef_at[step]]

        def finish(row, carry):
            total = jnp.where(group < LANES // 2 // chans, mixed[at(row), 0:LANES], mixed[at(row + 1), 0:LANES])
            total = total + pltpu.roll(total, LANES // 2, 1) + mixed[at(row + 2), LANES : 2 * LANES]
            value = keeps * state[at(row + 3), :] + adds * total
            if not is_last:
                value = jnp.where(inside(row + 3 - edge, LANES), value, 0.0)
            state[at(row), :] = value
            return carry

        lax.fori_loop(0, now_rows - 6, finish, 0)

    group = lax.broadcasted_iota(jnp.int32, (cols, LANES), 1) // chans
    packed = state[side : side + cols, :]
    for y in range(1, height):
        packed = jnp.where(group == y, state[y * stride + side : y * stride + side + cols, :], packed)
    half_send[...] = packed
    swap = remote(6, half_send, half_recv, partner)
    swap.start()
    swap.wait()
    other = half_recv[...]
    joined = jnp.concatenate(
        [jnp.where(first_core, packed, other), jnp.where(first_core, other, packed)], axis=0
    )
    flat = jnp.transpose(joined)
    for y in range(height):
        out_ref[y] = flat[y * chans : (y + 1) * chans]


def shards(
    latents, in_weight, mid_weight, out_weight, norm_mean, norm_rstd,
    cond_embed, time_embed, time_index, coef_index, sampler_table,
):
    chans, height, full_cols = latents.shape
    feat = in_weight.shape[3]
    steps = time_index.shape[0]
    margin = 3 * steps
    cols = full_cols // lax.axis_size("cfg")
    stride = up(cols + 2 * margin, 16)
    side = (stride - cols) // 2
    rows = height + 2 * margin
    wide = feat // TILE * TILE
    rest = feat - wide
    depth = 3 * wide + up(3 * rest, TILE)
    win = in_weight.reshape(9 * chans, feat)
    geom = (steps, height, full_cols, cols, stride, margin, feat, chans)
    whole = pl.BlockSpec(memory_space=pltpu.VMEM)
    scalars = pl.BlockSpec(memory_space=pltpu.SMEM)
    far = pl.BlockSpec(memory_space=pl.ANY)
    firsts = (rows - 2) * stride
    seconds = (rows - 4) * stride
    out = pl.pallas_call(
        functools.partial(section_kernel, geom),
        out_shape=jax.ShapeDtypeStruct((height, chans, full_cols), jnp.float32),
        in_specs=[scalars] * 3 + [whole, whole, far, whole, whole, whole, whole, far],
        out_specs=whole,
        scratch_shapes=[
            pltpu.VMEM((rows * stride, LANES), jnp.float32),
            pltpu.VMEM((6 * stride, 9 * chans), jnp.bfloat16),
            pltpu.VMEM((firsts, feat), jnp.float32),
            pltpu.VMEM((firsts, depth), jnp.bfloat16),
            pltpu.VMEM((firsts, depth), jnp.bfloat16),
            pltpu.VMEM((firsts, 3 * feat), jnp.float32),
            pltpu.VMEM((firsts, 3 * feat), jnp.float32),
            pltpu.VMEM((seconds, depth), jnp.bfloat16),
            pltpu.VMEM((rows * stride, 2 * LANES), jnp.float32),
            pltpu.VMEM(mid_weight.shape, mid_weight.dtype),
            pltpu.VMEM(time_embed.shape[::-1], time_embed.dtype),
            pltpu.VMEM((depth, 3 * feat), jnp.bfloat16),
            pltpu.VMEM((depth, 2 * LANES), jnp.bfloat16),
            pltpu.VMEM((up(2 + 4 * steps, 8), feat), jnp.float32),
            pltpu.VMEM((height * chans, full_cols), jnp.bfloat16),
            pltpu.VMEM((2 * margin * chans, full_cols), jnp.bfloat16),
            pltpu.VMEM((height * side, LANES), jnp.bfloat16),
            pltpu.VMEM((rows * side, LANES), jnp.bfloat16),
            pltpu.VMEM(cond_embed.shape, jnp.float32),
            pltpu.VMEM((cols, LANES), jnp.float32),
            pltpu.VMEM((cols, LANES), jnp.float32),
            pltpu.VMEM((stride, wide), jnp.int32),
            pltpu.SemaphoreType.DMA((2,)),
            pltpu.SemaphoreType.DMA((7,)),
            pltpu.SemaphoreType.DMA((7,)),
        ],
        compiler_params=pltpu.CompilerParams(
            vmem_limit_bytes=60 * 1024 * 1024, collective_id=0, has_side_effects=True
        ),
    )(
        time_index, coef_index, sampler_table, latents, win, mid_weight, out_weight,
        norm_mean, norm_rstd, cond_embed, time_embed.T,
    )
    return jnp.transpose(out, (1, 0, 2))


def solution(mesh):
    return jax.shard_map(
        shards,
        mesh=mesh,
        in_specs=(P("groups", "band", "sub"), P(), P(), P(), P(), P(), P("cfg", "groups"), P(), P(), P(), P()),
        out_specs=P("groups", "band", "sub"),
        check_vma=False,
    )
```

```python
import functools

import jax
import jax.numpy as jnp
from jax import lax
from jax.experimental import pallas as pl
from jax.experimental.pallas import tpu as pltpu
from jax.sharding import PartitionSpec as P

LANES = 128
TILE = 256
MESH = pl.DeviceIdType.MESH


def up(value, unit):
    return -(-value // unit) * unit


def turned(field, tap):
    return field if tap == 1 else pltpu.roll(field, (1 - tap) % field.shape[0], 0)


def section_kernel(
    geom, time_at, coef_at, table, lat_ref, win_ref, mid_hbm, wout_ref, mean_ref, rstd_ref, cond_ref, time_hbm, out_ref,
    state, taps, first, lift0, lift1, thin0, thin1, low, mixed,
    mid_ref, time_ref, wide_ref, narrow_ref, last_ref, vec_ref,
    row_send, row_recv, col_send, col_recv, cond_recv, half_send, half_recv, outside_ref,
    local_sem, send_sem, recv_sem,
):
    steps, height, full_cols, cols, stride, margin, feat, chans = geom
    wide = feat // TILE * TILE
    rest = feat - wide
    depth = 3 * wide + up(3 * rest, TILE)
    side = (stride - cols) // 2
    lifts = (lift0, lift1)
    thins = (thin0, thin1)
    band, sub, mine = (lax.axis_index(name) for name in ("band", "sub", "cfg"))
    bands, subs, parts = (lax.axis_size(name) for name in ("band", "sub", "cfg"))
    row_home = band * height
    image_rows = bands * height
    image_cols = subs * parts * cols
    col_home = (sub * parts + mine) * cols - side
    first_core = mine == 0

    place = lax.broadcasted_iota(jnp.int32, (stride, wide), 0) + col_home
    outside_ref[...] = jnp.where((place >= 0) & (place < image_cols), 0, 1)

    def inside(row, lanes):
        image_row = row_home + row
        limit = jnp.where((image_row >= 0) & (image_row < image_rows), 1, 0)
        return outside_ref[:, :lanes] < limit

    def at(row, count=1):
        return pl.ds(row * stride if isinstance(row, int) else pl.multiple_of(row * stride, 16), count * stride)

    ahead = jnp.where(first_core, sub + 1, sub - 1)
    behind = jnp.where(first_core, sub - 1, sub + 1)
    goes = (ahead >= 0) & (ahead < subs)
    comes = (behind >= 0) & (behind < subs)
    has_up = band > 0
    has_down = band < bands - 1
    partner = {"cfg": 1 - mine}

    mid_copy = pltpu.make_async_copy(mid_hbm, mid_ref, local_sem.at[0])
    time_copy = pltpu.make_async_copy(time_hbm, time_ref, local_sem.at[1])
    mid_copy.start()
    time_copy.start()

    barrier = pltpu.get_barrier_semaphore()

    def greet(when, device):
        @pl.when(when)
        def _():
            pl.semaphore_signal(barrier, inc=1, device_id=device, device_id_type=MESH)

    greet(has_up, {"band": band - 1})
    greet(has_down, {"band": band + 1})
    greet(comes, {"sub": behind})
    greet(comes & has_up, {"band": band - 1, "sub": behind})
    greet(comes & has_down, {"band": band + 1, "sub": behind})
    pl.semaphore_signal(barrier, inc=1, device_id=partner, device_id_type=MESH)

    copies = LANES // chans
    for y in range(height):
        row_send[y * chans : (y + 1) * chans, :] = lat_ref[:, y, :].astype(jnp.bfloat16)

    def stand(block):
        return jnp.transpose(jnp.concatenate([block] * copies, axis=0))

    def count(flag):
        return flag.astype(jnp.int32)

    pl.semaphore_wait(
        barrier,
        1 + count(has_up) + count(has_down) + count(goes) + count(goes & has_up) + count(goes & has_down),
    )

    rows = height + 2 * margin
    row_part = margin * chans
    col_part = margin * side

    def remote(k, source, target, device):
        return pltpu.make_async_remote_copy(
            src_ref=source, dst_ref=target, send_sem=send_sem.at[k], recv_sem=recv_sem.at[k],
            device_id=device, device_id_type=MESH,
        )

    row_all = height * chans
    col_all = height * side
    sends = [
        (has_down, has_up, remote(0, row_send.at[row_all - row_part : row_all], row_recv.at[0:row_part], {"band": band + 1})),
        (has_up, has_down, remote(1, row_send.at[0:row_part], row_recv.at[row_part : 2 * row_part], {"band": band - 1})),
        (goes, comes, remote(2, col_send, col_recv.at[col_part : col_part + col_all], {"sub": ahead})),
        (goes & has_down, comes & has_up, remote(3, col_send.at[col_all - col_part : col_all], col_recv.at[0:col_part], {"band": band + 1, "sub": ahead})),
        (goes & has_up, comes & has_down, remote(4, col_send.at[0:col_part], col_recv.at[col_part + col_all : 2 * col_part + col_all], {"band": band - 1, "sub": ahead})),
    ]
    for go, come, copy in sends[:2]:
        pl.when(go)(copy.start)
    cond_copy = remote(5, cond_ref, cond_recv, partner)
    cond_copy.start()

    bodies = [stand(lat_ref[:, y, :]) for y in range(height)]
    for y in range(0, height, 2):
        pair = [
            jnp.where(first_core, bodies[y + k][full_cols - side :], bodies[y + k][:side]) for k in range(2)
        ]
        col_send[y * side : (y + 2) * side, :] = jnp.concatenate(pair, axis=0).astype(jnp.bfloat16)

    for go, come, copy in sends[2:]:
        pl.when(go)(copy.start)

    mid_copy.wait()
    for i in range(3):
        for j in range(3):
            turned_mid = jnp.transpose(mid_ref[i, j])
            base = i * depth
            wide_ref[base + j * wide : base + (j + 1) * wide, :] = turned_mid[:wide, :wide]
            narrow_ref[j * wide : (j + 1) * wide, i * rest : (i + 1) * rest] = turned_mid[:wide, wide:]
            spot = 3 * wide + j * rest
            wide_ref[base + spot : base + spot + rest, :] = turned_mid[wide:, :wide]
            narrow_ref[spot : spot + rest, i * rest : (i + 1) * rest] = turned_mid[wide:, wide:]
            small = wout_ref[i, j].astype(jnp.float32)
            tall = jnp.transpose(jnp.concatenate([small] * copies, axis=0)).astype(jnp.bfloat16)
            span = slice(i * LANES // 2, (i + 1) * LANES // 2) if i < 2 else slice(LANES, 2 * LANES)
            tall = tall[:, : span.stop - span.start]
            last_ref[j * wide : (j + 1) * wide, span] = tall[:wide]
            last_ref[spot : spot + rest, span] = tall[wide:]
        spare = 3 * wide + 3 * rest
        wide_ref[i * depth + spare : (i + 1) * depth, :] = jnp.zeros((depth - spare, wide), jnp.bfloat16)
    narrow_ref[spare:, :] = jnp.zeros((depth - spare, 3 * rest), jnp.bfloat16)
    last_ref[spare:, :] = jnp.zeros((depth - spare, 2 * LANES), jnp.bfloat16)

    cond_copy.wait()
    time_copy.wait()
    plain = jnp.where(first_core, cond_ref[...], cond_recv[...])
    steered = jnp.where(first_core, cond_recv[...], cond_ref[...])
    half_rstd = 0.5 * rstd_ref[...]
    vec_ref[0:2, :] = half_rstd
    moments = lax.broadcasted_iota(jnp.int32, time_ref.shape, 1)
    for step in range(steps):
        column = jnp.sum(jnp.where(moments == time_at[step], time_ref[...], 0.0), axis=1, keepdims=True)
        time_row = jnp.transpose(jnp.broadcast_to(column, (feat, LANES)))[0:1]
        for layer in range(2):
            for q, cond in enumerate((plain, steered)):
                line = 2 + 4 * step + 2 * layer + q
                vec_ref[line : line + 1, :] = (time_row + cond - mean_ref[layer : layer + 1, :]) * half_rstd[layer : layer + 1, :]

    def wait_for(copy):
        def both():
            copy.wait_recv()

        return both

    for go, come, copy in sends:
        pl.when(go)(copy.wait_send)
        pl.when(come)(wait_for(copy))

    for row in range(rows):
        if margin <= row < margin + height:
            body = bodies[row - margin]
        else:
            spot = row if row < margin else row - height
            body = stand(row_recv[spot * chans : (spot + 1) * chans, :].astype(jnp.float32))
        pair = col_recv[row // 2 * 2 * side : (row // 2 * 2 + 2) * side, :].astype(jnp.float32)
        border = pair[row % 2 * side : (row % 2 + 1) * side]
        field = jnp.where(
            first_core,
            jnp.concatenate([border, body[: cols + side]], axis=0),
            jnp.concatenate([body[full_cols - cols - side :], border], axis=0),
        )
        state[row * stride : (row + 1) * stride, :] = jnp.where(inside(row - margin, LANES), field, 0.0)

    group = lax.broadcasted_iota(jnp.int32, (stride, LANES), 1) // chans

    def silu_of(half):
        return half + half * jnp.tanh(half)

    def spread(ref, row, big, small):
        for tap in range(3):
            ref[at(row), tap * wide : (tap + 1) * wide] = turned(big, tap).astype(jnp.bfloat16)
        ends = [turned(small, tap) for tap in range(3)]
        ends.append(jnp.zeros((stride, depth - 3 * wide - 3 * rest), jnp.float32))
        ref[at(row), 3 * wide : depth] = jnp.concatenate(ends, axis=1).astype(jnp.bfloat16)

    for step in range(steps):
        edge = margin - 3 * step
        now_rows = height + 2 * edge
        firsts = now_rows - 2
        seconds = now_rows - 4
        is_last = step == steps - 1
        base = 2 + 4 * step

        def lay(row, carry):
            field = state[at(row), :]
            before = turned(field, 0)
            after = turned(field, 2)
            mixed[at(row), 0:LANES] = jnp.where(group % 3 == 0, before, jnp.where(group % 3 == 1, field, after))
            mixed[at(row), LANES : 2 * LANES] = after
            return carry

        lax.fori_loop(0, now_rows, lay, 0, unroll=True)

        chunk = 6 if firsts % 6 == 0 else 2

        def lead(k, carry):
            row = k * chunk
            for m in range(chunk):
                one = mixed[at(row + m), 0:LANES]
                two = mixed[at(row + m + 1), 0:LANES]
                three = mixed[at(row + m + 2), 0:LANES]
                body = jnp.where(group < 3, one, jnp.where(group < 6, two, three))
                taps[at(m), 0:LANES] = body.astype(jnp.bfloat16)
                taps[at(m), LANES : LANES + chans] = mixed[at(row + m + 2), LANES : LANES + chans].astype(jnp.bfloat16)
            field = jnp.dot(taps[...][: chunk * stride], win_ref[...], preferred_element_type=jnp.float32)
            first[at(row, chunk), :] = field
            for q in range(2):
                shift = vec_ref[base + q : base + q + 1, :]
                for m in range(chunk):
                    here = field[m * stride : (m + 1) * stride]
                    keep = inside(row + m + 1 - edge, wide)
                    parts = []
                    for part in (slice(0, wide), slice(wide, feat)):
                        value = silu_of(here[:, part] * vec_ref[0:1, part] + shift[:, part])
                        parts.append(jnp.where(keep[:, : value.shape[1]], value, 0.0))
                    spread(lifts[q], row + m, *parts)
                thins[q][at(row, chunk), :] = jnp.dot(
                    lifts[q][at(row, chunk), :], narrow_ref[...], preferred_element_type=jnp.float32
                )
            return carry

        lax.fori_loop(0, firsts // chunk, lead, 0, unroll=True)

        count2 = 8 if seconds % 8 == 0 else (10 if seconds % 10 == 0 else 2)
        gain = table[2, coef_at[step]]

        def middle(k, carry):
            row = k * count2
            found = []
            for q in range(2):
                window = jnp.concatenate([lifts[q][at(row + tap, count2), :] for tap in range(3)], axis=1)
                total = first[at(row + 1, count2), 0:wide] + jnp.dot(
                    window, wide_ref[...], preferred_element_type=jnp.float32
                )
                tail = first[at(row + 1, count2), wide:feat]
                for tap in range(3):
                    tail = tail + thins[q][at(row + tap, count2), tap * rest : (tap + 1) * rest]
                shift = vec_ref[base + 2 + q : base + 3 + q, :]
                found.append(
                    [
                        silu_of(field * vec_ref[1:2, part] + shift[:, part])
                        for field, part in ((total, slice(0, wide)), (tail, slice(wide, feat)))
                    ]
                )
            lowered = [a + gain * (b - a) for a, b in zip(*found)]
            for m in range(count2):
                keep = inside(row + m + 2 - edge, wide)
                spread(
                    low,
                    row + m,
                    *[
                        jnp.where(keep[:, : part.shape[1]], part[m * stride : (m + 1) * stride], 0.0)
                        for part in lowered
                    ],
                )
            mixed[at(row, count2), :] = jnp.dot(low[at(row, count2), :], last_ref[...], preferred_element_type=jnp.float32)
            return carry

        lax.fori_loop(0, seconds // count2, middle, 0, unroll=True)

        keeps = table[0, coef_at[step]]
        adds = table[1, coef_at[step]]

        def finish(row, carry):
            total = jnp.where(group < LANES // 2 // chans, mixed[at(row), 0:LANES], mixed[at(row + 1), 0:LANES])
            total = total + pltpu.roll(total, LANES // 2, 1) + mixed[at(row + 2), LANES : 2 * LANES]
            value = keeps * state[at(row + 3), :] + adds * total
            if not is_last:
                value = jnp.where(inside(row + 3 - edge, LANES), value, 0.0)
            state[at(row), :] = value
            return carry

        lax.fori_loop(0, now_rows - 6, finish, 0, unroll=True)

    group = lax.broadcasted_iota(jnp.int32, (cols, LANES), 1) // chans
    packed = state[side : side + cols, :]
    for y in range(1, height):
        packed = jnp.where(group == y, state[y * stride + side : y * stride + side + cols, :], packed)
    half_send[...] = packed
    swap = remote(6, half_send, half_recv, partner)
    swap.start()
    swap.wait()
    other = half_recv[...]
    joined = jnp.concatenate(
        [jnp.where(first_core, packed, other), jnp.where(first_core, other, packed)], axis=0
    )
    flat = jnp.transpose(joined)
    for y in range(height):
        out_ref[y] = flat[y * chans : (y + 1) * chans]


def shards(
    latents, in_weight, mid_weight, out_weight, norm_mean, norm_rstd,
    cond_embed, time_embed, time_index, coef_index, sampler_table,
):
    chans, height, full_cols = latents.shape
    feat = in_weight.shape[3]
    steps = time_index.shape[0]
    margin = 3 * steps
    cols = full_cols // lax.axis_size("cfg")
    stride = up(cols + 2 * margin, 16)
    side = (stride - cols) // 2
    rows = height + 2 * margin
    wide = feat // TILE * TILE
    rest = feat - wide
    depth = 3 * wide + up(3 * rest, TILE)
    win = in_weight.reshape(9 * chans, feat)
    geom = (steps, height, full_cols, cols, stride, margin, feat, chans)
    whole = pl.BlockSpec(memory_space=pltpu.VMEM)
    scalars = pl.BlockSpec(memory_space=pltpu.SMEM)
    far = pl.BlockSpec(memory_space=pl.ANY)
    firsts = (rows - 2) * stride
    seconds = (rows - 4) * stride
    out = pl.pallas_call(
        functools.partial(section_kernel, geom),
        out_shape=jax.ShapeDtypeStruct((height, chans, full_cols), jnp.float32),
        in_specs=[scalars] * 3 + [whole, whole, far, whole, whole, whole, whole, far],
        out_specs=whole,
        scratch_shapes=[
            pltpu.VMEM((rows * stride, LANES), jnp.float32),
            pltpu.VMEM((6 * stride, 9 * chans), jnp.bfloat16),
            pltpu.VMEM((firsts, feat), jnp.float32),
            pltpu.VMEM((firsts, depth), jnp.bfloat16),
            pltpu.VMEM((firsts, depth), jnp.bfloat16),
            pltpu.VMEM((firsts, 3 * rest), jnp.float32),
            pltpu.VMEM((firsts, 3 * rest), jnp.float32),
            pltpu.VMEM((seconds, depth), jnp.bfloat16),
            pltpu.VMEM((rows * stride, 2 * LANES), jnp.float32),
            pltpu.VMEM(mid_weight.shape, mid_weight.dtype),
            pltpu.VMEM(time_embed.shape[::-1], time_embed.dtype),
            pltpu.VMEM((3 * depth, wide), jnp.bfloat16),
            pltpu.VMEM((depth, 3 * rest), jnp.bfloat16),
            pltpu.VMEM((depth, 2 * LANES), jnp.bfloat16),
            pltpu.VMEM((up(2 + 4 * steps, 8), feat), jnp.float32),
            pltpu.VMEM((height * chans, full_cols), jnp.bfloat16),
            pltpu.VMEM((2 * margin * chans, full_cols), jnp.bfloat16),
            pltpu.VMEM((height * side, LANES), jnp.bfloat16),
            pltpu.VMEM((rows * side, LANES), jnp.bfloat16),
            pltpu.VMEM(cond_embed.shape, jnp.float32),
            pltpu.VMEM((cols, LANES), jnp.float32),
            pltpu.VMEM((cols, LANES), jnp.float32),
            pltpu.VMEM((stride, wide), jnp.int32),
            pltpu.SemaphoreType.DMA((2,)),
            pltpu.SemaphoreType.DMA((7,)),
            pltpu.SemaphoreType.DMA((7,)),
        ],
        compiler_params=pltpu.CompilerParams(
            vmem_limit_bytes=60 * 1024 * 1024, collective_id=0, has_side_effects=True
        ),
    )(
        time_index, coef_index, sampler_table, latents, win, mid_weight, out_weight,
        norm_mean, norm_rstd, cond_embed, time_embed.T,
    )
    return jnp.transpose(out, (1, 0, 2))


def solution(mesh):
    return jax.shard_map(
        shards,
        mesh=mesh,
        in_specs=(P("groups", "band", "sub"), P(), P(), P(), P(), P(), P("cfg", "groups"), P(), P(), P(), P()),
        out_specs=P("groups", "band", "sub"),
        check_vma=False,
    )
```

```python
import functools

import jax
import jax.numpy as jnp
from jax import lax
from jax.experimental import pallas as pl
from jax.experimental.pallas import tpu as pltpu
from jax.sharding import PartitionSpec as P

LANES = 128
TILE = 256
MESH = pl.DeviceIdType.MESH


def up(value, unit):
    return -(-value // unit) * unit


def turned(field, tap):
    return field if tap == 1 else pltpu.roll(field, (1 - tap) % field.shape[0], 0)


def section_kernel(
    geom, time_at, coef_at, table, lat_ref, win_ref, mid_hbm, wout_ref, mean_ref, rstd_ref, cond_ref, time_hbm, out_ref,
    state, taps, first, lift0, lift1, thin0, thin1, low, mixed, noise,
    mid_ref, time_ref, wide_ref, narrow_ref, last_ref, vec_ref,
    row_send, row_recv, col_send, col_recv, cond_recv, half_send, half_recv, outside_ref,
    local_sem, send_sem, recv_sem,
):
    steps, height, full_cols, cols, stride, margin, feat, chans = geom
    wide = feat // TILE * TILE
    rest = feat - wide
    depth = 3 * wide + up(3 * rest, TILE)
    side = (stride - cols) // 2
    lifts = (lift0, lift1)
    thins = (thin0, thin1)
    band, sub, mine = (lax.axis_index(name) for name in ("band", "sub", "cfg"))
    bands, subs, parts = (lax.axis_size(name) for name in ("band", "sub", "cfg"))
    row_home = band * height
    image_rows = bands * height
    image_cols = subs * parts * cols
    col_home = (sub * parts + mine) * cols - side
    first_core = mine == 0

    place = lax.broadcasted_iota(jnp.int32, (stride, wide), 0) + col_home
    outside_ref[...] = jnp.where((place >= 0) & (place < image_cols), 0, 1)

    def inside(row, lanes):
        image_row = row_home + row
        limit = jnp.where((image_row >= 0) & (image_row < image_rows), 1, 0)
        return outside_ref[:, :lanes] < limit

    def at(row, count=1):
        return pl.ds(row * stride if isinstance(row, int) else pl.multiple_of(row * stride, 16), count * stride)

    ahead = jnp.where(first_core, sub + 1, sub - 1)
    behind = jnp.where(first_core, sub - 1, sub + 1)
    goes = (ahead >= 0) & (ahead < subs)
    comes = (behind >= 0) & (behind < subs)
    has_up = band > 0
    has_down = band < bands - 1
    partner = {"cfg": 1 - mine}

    mid_copy = pltpu.make_async_copy(mid_hbm, mid_ref, local_sem.at[0])
    time_copy = pltpu.make_async_copy(time_hbm, time_ref, local_sem.at[1])
    mid_copy.start()
    time_copy.start()

    barrier = pltpu.get_barrier_semaphore()

    def greet(when, device):
        @pl.when(when)
        def _():
            pl.semaphore_signal(barrier, inc=1, device_id=device, device_id_type=MESH)

    greet(has_up, {"band": band - 1})
    greet(has_down, {"band": band + 1})
    greet(comes, {"sub": behind})
    greet(comes & has_up, {"band": band - 1, "sub": behind})
    greet(comes & has_down, {"band": band + 1, "sub": behind})
    pl.semaphore_signal(barrier, inc=1, device_id=partner, device_id_type=MESH)

    copies = LANES // chans
    for y in range(height):
        row_send[y * chans : (y + 1) * chans, :] = lat_ref[:, y, :].astype(jnp.bfloat16)

    def stand(block):
        return jnp.transpose(jnp.concatenate([block] * copies, axis=0))

    def count(flag):
        return flag.astype(jnp.int32)

    pl.semaphore_wait(
        barrier,
        1 + count(has_up) + count(has_down) + count(goes) + count(goes & has_up) + count(goes & has_down),
    )

    rows = height + 2 * margin
    row_part = margin * chans
    col_part = margin * side

    def remote(k, source, target, device):
        return pltpu.make_async_remote_copy(
            src_ref=source, dst_ref=target, send_sem=send_sem.at[k], recv_sem=recv_sem.at[k],
            device_id=device, device_id_type=MESH,
        )

    row_all = height * chans
    col_all = height * side
    sends = [
        (has_down, has_up, remote(0, row_send.at[row_all - row_part : row_all], row_recv.at[0:row_part], {"band": band + 1})),
        (has_up, has_down, remote(1, row_send.at[0:row_part], row_recv.at[row_part : 2 * row_part], {"band": band - 1})),
        (goes, comes, remote(2, col_send, col_recv.at[col_part : col_part + col_all], {"sub": ahead})),
        (goes & has_down, comes & has_up, remote(3, col_send.at[col_all - col_part : col_all], col_recv.at[0:col_part], {"band": band + 1, "sub": ahead})),
        (goes & has_up, comes & has_down, remote(4, col_send.at[0:col_part], col_recv.at[col_part + col_all : 2 * col_part + col_all], {"band": band - 1, "sub": ahead})),
    ]
    for go, come, copy in sends[:2]:
        pl.when(go)(copy.start)
    cond_copy = remote(5, cond_ref, cond_recv, partner)
    cond_copy.start()

    bodies = [stand(lat_ref[:, y, :]) for y in range(height)]
    for y in range(0, height, 2):
        pair = [
            jnp.where(first_core, bodies[y + k][full_cols - side :], bodies[y + k][:side]) for k in range(2)
        ]
        col_send[y * side : (y + 2) * side, :] = jnp.concatenate(pair, axis=0).astype(jnp.bfloat16)

    for go, come, copy in sends[2:]:
        pl.when(go)(copy.start)

    mid_copy.wait()
    for i in range(3):
        for j in range(3):
            turned_mid = jnp.transpose(mid_ref[i, j])
            base = i * depth
            wide_ref[base + j * wide : base + (j + 1) * wide, :] = turned_mid[:wide, :wide]
            narrow_ref[j * wide : (j + 1) * wide, i * rest : (i + 1) * rest] = turned_mid[:wide, wide:]
            spot = 3 * wide + j * rest
            wide_ref[base + spot : base + spot + rest, :] = turned_mid[wide:, :wide]
            narrow_ref[spot : spot + rest, i * rest : (i + 1) * rest] = turned_mid[wide:, wide:]
            small = wout_ref[i, j].astype(jnp.float32)
            tall = jnp.transpose(jnp.concatenate([small] * copies, axis=0)).astype(jnp.bfloat16)
            span = slice(i * LANES // 2, (i + 1) * LANES // 2) if i < 2 else slice(LANES, 2 * LANES)
            tall = tall[:, : span.stop - span.start]
            last_ref[j * wide : (j + 1) * wide, span] = tall[:wide]
            last_ref[spot : spot + rest, span] = tall[wide:]
        spare = 3 * wide + 3 * rest
        wide_ref[i * depth + spare : (i + 1) * depth, :] = jnp.zeros((depth - spare, wide), jnp.bfloat16)
    narrow_ref[spare:, :] = jnp.zeros((depth - spare, 3 * rest), jnp.bfloat16)
    last_ref[spare:, :] = jnp.zeros((depth - spare, 2 * LANES), jnp.bfloat16)

    cond_copy.wait()
    time_copy.wait()
    plain = jnp.where(first_core, cond_ref[...], cond_recv[...])
    steered = jnp.where(first_core, cond_recv[...], cond_ref[...])
    half_rstd = 0.5 * rstd_ref[...]
    vec_ref[0:2, :] = half_rstd
    moments = lax.broadcasted_iota(jnp.int32, time_ref.shape, 1)
    for step in range(steps):
        column = jnp.sum(jnp.where(moments == time_at[step], time_ref[...], 0.0), axis=1, keepdims=True)
        time_row = jnp.transpose(jnp.broadcast_to(column, (feat, LANES)))[0:1]
        for layer in range(2):
            for q, cond in enumerate((plain, steered)):
                line = 2 + 4 * step + 2 * layer + q
                vec_ref[line : line + 1, :] = (time_row + cond - mean_ref[layer : layer + 1, :]) * half_rstd[layer : layer + 1, :]

    def wait_for(copy):
        def both():
            copy.wait_recv()

        return both

    for go, come, copy in sends:
        pl.when(go)(copy.wait_send)
        pl.when(come)(wait_for(copy))

    for row in range(rows):
        if margin <= row < margin + height:
            body = bodies[row - margin]
        else:
            spot = row if row < margin else row - height
            body = stand(row_recv[spot * chans : (spot + 1) * chans, :].astype(jnp.float32))
        pair = col_recv[row // 2 * 2 * side : (row // 2 * 2 + 2) * side, :].astype(jnp.float32)
        border = pair[row % 2 * side : (row % 2 + 1) * side]
        field = jnp.where(
            first_core,
            jnp.concatenate([border, body[: cols + side]], axis=0),
            jnp.concatenate([body[full_cols - cols - side :], border], axis=0),
        )
        state[row * stride : (row + 1) * stride, :] = jnp.where(inside(row - margin, LANES), field, 0.0)

    group = lax.broadcasted_iota(jnp.int32, (stride, LANES), 1) // chans

    def silu_of(half):
        return half + half * jnp.tanh(half)

    def spread(ref, row, big, small):
        for tap in range(3):
            ref[at(row), tap * wide : (tap + 1) * wide] = turned(big, tap).astype(jnp.bfloat16)
        ends = [turned(small, tap) for tap in range(3)]
        ends.append(jnp.zeros((stride, depth - 3 * wide - 3 * rest), jnp.float32))
        ref[at(row), 3 * wide : depth] = jnp.concatenate(ends, axis=1).astype(jnp.bfloat16)

    for step in range(steps):
        edge = margin - 3 * step
        now_rows = height + 2 * edge
        firsts = now_rows - 2
        seconds = now_rows - 4
        is_last = step == steps - 1
        base = 2 + 4 * step

        def lay(row, carry):
            field = state[at(row), :]
            before = turned(field, 0)
            after = turned(field, 2)
            mixed[at(row), 0:LANES] = jnp.where(group % 3 == 0, before, jnp.where(group % 3 == 1, field, after))
            mixed[at(row), LANES : 2 * LANES] = after
            return carry

        lax.fori_loop(0, now_rows, lay, 0, unroll=True)

        chunk = 6 if firsts % 6 == 0 else 2

        def lead(k, carry):
            row = k * chunk
            for m in range(chunk):
                one = mixed[at(row + m), 0:LANES]
                two = mixed[at(row + m + 1), 0:LANES]
                three = mixed[at(row + m + 2), 0:LANES]
                body = jnp.where(group < 3, one, jnp.where(group < 6, two, three))
                taps[at(row + m), 0:LANES] = body.astype(jnp.bfloat16)
                taps[at(row + m), LANES : LANES + chans] = mixed[at(row + m + 2), LANES : LANES + chans].astype(jnp.bfloat16)
            field = jnp.dot(taps[at(row, chunk), :], win_ref[...], preferred_element_type=jnp.float32)
            first[at(row, chunk), :] = field
            for q in range(2):
                shift = vec_ref[base + q : base + q + 1, :]
                for m in range(chunk):
                    here = field[m * stride : (m + 1) * stride]
                    keep = inside(row + m + 1 - edge, wide)
                    parts = []
                    for part in (slice(0, wide), slice(wide, feat)):
                        value = silu_of(here[:, part] * vec_ref[0:1, part] + shift[:, part])
                        parts.append(jnp.where(keep[:, : value.shape[1]], value, 0.0))
                    spread(lifts[q], row + m, *parts)
                thins[q][at(row, chunk), :] = jnp.dot(
                    lifts[q][at(row, chunk), :], narrow_ref[...], preferred_element_type=jnp.float32
                )
            return carry

        lax.fori_loop(0, firsts // chunk, lead, 0, unroll=True)

        count2 = 8 if seconds % 8 == 0 else (5 if seconds % 5 == 0 else 2)
        gain = table[2, coef_at[step]]

        def middle(k, carry):
            row = k * count2
            found = []
            for q in range(2):
                window = jnp.concatenate([lifts[q][at(row + tap, count2), :] for tap in range(3)], axis=1)
                total = first[at(row + 1, count2), 0:wide] + jnp.dot(
                    window, wide_ref[...], preferred_element_type=jnp.float32
                )
                tail = first[at(row + 1, count2), wide:feat]
                for tap in range(3):
                    tail = tail + thins[q][at(row + tap, count2), tap * rest : (tap + 1) * rest]
                shift = vec_ref[base + 2 + q : base + 3 + q, :]
                found.append(
                    [
                        silu_of(field * vec_ref[1:2, part] + shift[:, part])
                        for field, part in ((total, slice(0, wide)), (tail, slice(wide, feat)))
                    ]
                )
            lowered = [a + gain * (b - a) for a, b in zip(*found)]
            for m in range(count2):
                keep = inside(row + m + 2 - edge, wide)
                spread(
                    low,
                    row + m,
                    *[
                        jnp.where(keep[:, : part.shape[1]], part[m * stride : (m + 1) * stride], 0.0)
                        for part in lowered
                    ],
                )
            noise[at(row, count2), :] = jnp.dot(low[at(row, count2), :], last_ref[...], preferred_element_type=jnp.float32)
            return carry

        lax.fori_loop(0, seconds // count2, middle, 0, unroll=True)

        keeps = table[0, coef_at[step]]
        adds = table[1, coef_at[step]]

        def finish(row, carry):
            total = jnp.where(group < LANES // 2 // chans, noise[at(row), 0:LANES], noise[at(row + 1), 0:LANES])
            total = total + pltpu.roll(total, LANES // 2, 1) + noise[at(row + 2), LANES : 2 * LANES]
            value = keeps * state[at(row + 3), :] + adds * total
            if not is_last:
                value = jnp.where(inside(row + 3 - edge, LANES), value, 0.0)
            state[at(row), :] = value
            return carry

        lax.fori_loop(0, now_rows - 6, finish, 0, unroll=True)

    group = lax.broadcasted_iota(jnp.int32, (cols, LANES), 1) // chans
    packed = state[side : side + cols, :]
    for y in range(1, height):
        packed = jnp.where(group == y, state[y * stride + side : y * stride + side + cols, :], packed)
    half_send[...] = packed
    swap = remote(6, half_send, half_recv, partner)
    swap.start()
    swap.wait()
    other = half_recv[...]
    joined = jnp.concatenate(
        [jnp.where(first_core, packed, other), jnp.where(first_core, other, packed)], axis=0
    )
    flat = jnp.transpose(joined)
    for y in range(height):
        out_ref[y] = flat[y * chans : (y + 1) * chans]


def shards(
    latents, in_weight, mid_weight, out_weight, norm_mean, norm_rstd,
    cond_embed, time_embed, time_index, coef_index, sampler_table,
):
    chans, height, full_cols = latents.shape
    feat = in_weight.shape[3]
    steps = time_index.shape[0]
    margin = 3 * steps
    cols = full_cols // lax.axis_size("cfg")
    stride = up(cols + 2 * margin, 16)
    side = (stride - cols) // 2
    rows = height + 2 * margin
    wide = feat // TILE * TILE
    rest = feat - wide
    depth = 3 * wide + up(3 * rest, TILE)
    win = in_weight.reshape(9 * chans, feat)
    geom = (steps, height, full_cols, cols, stride, margin, feat, chans)
    whole = pl.BlockSpec(memory_space=pltpu.VMEM)
    scalars = pl.BlockSpec(memory_space=pltpu.SMEM)
    far = pl.BlockSpec(memory_space=pl.ANY)
    firsts = (rows - 2) * stride
    seconds = (rows - 4) * stride
    out = pl.pallas_call(
        functools.partial(section_kernel, geom),
        out_shape=jax.ShapeDtypeStruct((height, chans, full_cols), jnp.float32),
        in_specs=[scalars] * 3 + [whole, whole, far, whole, whole, whole, whole, far],
        out_specs=whole,
        scratch_shapes=[
            pltpu.VMEM((rows * stride, LANES), jnp.float32),
            pltpu.VMEM((firsts, 9 * chans), jnp.bfloat16),
            pltpu.VMEM((firsts, feat), jnp.float32),
            pltpu.VMEM((firsts, depth), jnp.bfloat16),
            pltpu.VMEM((firsts, depth), jnp.bfloat16),
            pltpu.VMEM((firsts, 3 * rest), jnp.float32),
            pltpu.VMEM((firsts, 3 * rest), jnp.float32),
            pltpu.VMEM((seconds, depth), jnp.bfloat16),
            pltpu.VMEM((rows * stride, 2 * LANES), jnp.float32),
            pltpu.VMEM((seconds, 2 * LANES), jnp.float32),
            pltpu.VMEM(mid_weight.shape, mid_weight.dtype),
            pltpu.VMEM(time_embed.shape[::-1], time_embed.dtype),
            pltpu.VMEM((3 * depth, wide), jnp.bfloat16),
            pltpu.VMEM((depth, 3 * rest), jnp.bfloat16),
            pltpu.VMEM((depth, 2 * LANES), jnp.bfloat16),
            pltpu.VMEM((up(2 + 4 * steps, 8), feat), jnp.float32),
            pltpu.VMEM((height * chans, full_cols), jnp.bfloat16),
            pltpu.VMEM((2 * margin * chans, full_cols), jnp.bfloat16),
            pltpu.VMEM((height * side, LANES), jnp.bfloat16),
            pltpu.VMEM((rows * side, LANES), jnp.bfloat16),
            pltpu.VMEM(cond_embed.shape, jnp.float32),
            pltpu.VMEM((cols, LANES), jnp.float32),
            pltpu.VMEM((cols, LANES), jnp.float32),
            pltpu.VMEM((stride, wide), jnp.int32),
            pltpu.SemaphoreType.DMA((2,)),
            pltpu.SemaphoreType.DMA((7,)),
            pltpu.SemaphoreType.DMA((7,)),
        ],
        compiler_params=pltpu.CompilerParams(
            vmem_limit_bytes=54 * 1024 * 1024, collective_id=0, has_side_effects=True
        ),
    )(
        time_index, coef_index, sampler_table, latents, win, mid_weight, out_weight,
        norm_mean, norm_rstd, cond_embed, time_embed.T,
    )
    return jnp.transpose(out, (1, 0, 2))


def solution(mesh):
    return jax.shard_map(
        shards,
        mesh=mesh,
        in_specs=(P("groups", "band", "sub"), P(), P(), P(), P(), P(), P("cfg", "groups"), P(), P(), P(), P()),
        out_specs=P("groups", "band", "sub"),
        check_vma=False,
    )
```

```python
import functools

import jax
import jax.numpy as jnp
from jax import lax
from jax.experimental import pallas as pl
from jax.experimental.pallas import tpu as pltpu
from jax.sharding import PartitionSpec as P

LANES = 128
TILE = 256
MESH = pl.DeviceIdType.MESH


def up(value, unit):
    return -(-value // unit) * unit


def turned(field, tap):
    return field if tap == 1 else pltpu.roll(field, (1 - tap) % field.shape[0], 0)


def section_kernel(
    geom, time_at, coef_at, table, lat_ref, win_ref, mid_hbm, wout_ref, mean_ref, rstd_ref, cond_ref, time_hbm, out_ref,
    state, taps, first, lift0, lift1, thin0, thin1, low, mixed, noise,
    mid_ref, time_ref, wide_ref, narrow_ref, last_ref, vec_ref,
    row_send, row_recv, col_send, col_recv, cond_recv, half_send, half_recv, outside_ref,
    local_sem, send_sem, recv_sem,
):
    steps, height, full_cols, cols, stride, margin, feat, chans = geom
    wide = feat // TILE * TILE
    rest = feat - wide
    depth = 3 * wide + up(3 * rest, TILE)
    side = (stride - cols) // 2
    lifts = (lift0, lift1)
    thins = (thin0, thin1)
    band, sub, mine = (lax.axis_index(name) for name in ("band", "sub", "cfg"))
    bands, subs, parts = (lax.axis_size(name) for name in ("band", "sub", "cfg"))
    row_home = band * height
    image_rows = bands * height
    image_cols = subs * parts * cols
    col_home = (sub * parts + mine) * cols - side
    first_core = mine == 0

    place = lax.broadcasted_iota(jnp.int32, (stride, wide), 0) + col_home
    outside_ref[...] = jnp.where((place >= 0) & (place < image_cols), 0, 1)

    def inside(row, lanes):
        image_row = row_home + row
        limit = jnp.where((image_row >= 0) & (image_row < image_rows), 1, 0)
        return outside_ref[:, :lanes] < limit

    def at(row, count=1):
        return pl.ds(row * stride if isinstance(row, int) else pl.multiple_of(row * stride, 16), count * stride)

    ahead = jnp.where(first_core, sub + 1, sub - 1)
    behind = jnp.where(first_core, sub - 1, sub + 1)
    goes = (ahead >= 0) & (ahead < subs)
    comes = (behind >= 0) & (behind < subs)
    has_up = band > 0
    has_down = band < bands - 1
    partner = {"cfg": 1 - mine}

    mid_copy = pltpu.make_async_copy(mid_hbm, mid_ref, local_sem.at[0])
    time_copy = pltpu.make_async_copy(time_hbm, time_ref, local_sem.at[1])
    mid_copy.start()
    time_copy.start()

    barrier = pltpu.get_barrier_semaphore()

    def greet(when, device):
        @pl.when(when)
        def _():
            pl.semaphore_signal(barrier, inc=1, device_id=device, device_id_type=MESH)

    greet(has_up, {"band": band - 1})
    greet(has_down, {"band": band + 1})
    greet(comes, {"sub": behind})
    greet(comes & has_up, {"band": band - 1, "sub": behind})
    greet(comes & has_down, {"band": band + 1, "sub": behind})
    pl.semaphore_signal(barrier, inc=1, device_id=partner, device_id_type=MESH)

    copies = LANES // chans
    for y in range(height):
        row_send[y * chans : (y + 1) * chans, :] = lat_ref[:, y, :].astype(jnp.bfloat16)

    def stand(block):
        return jnp.transpose(jnp.concatenate([block] * copies, axis=0))

    def count(flag):
        return flag.astype(jnp.int32)

    pl.semaphore_wait(
        barrier,
        1 + count(has_up) + count(has_down) + count(goes) + count(goes & has_up) + count(goes & has_down),
    )

    rows = height + 2 * margin
    row_part = margin * chans
    col_part = margin * side

    def remote(k, source, target, device):
        return pltpu.make_async_remote_copy(
            src_ref=source, dst_ref=target, send_sem=send_sem.at[k], recv_sem=recv_sem.at[k],
            device_id=device, device_id_type=MESH,
        )

    row_all = height * chans
    col_all = height * side
    sends = [
        (has_down, has_up, remote(0, row_send.at[row_all - row_part : row_all], row_recv.at[0:row_part], {"band": band + 1})),
        (has_up, has_down, remote(1, row_send.at[0:row_part], row_recv.at[row_part : 2 * row_part], {"band": band - 1})),
        (goes, comes, remote(2, col_send, col_recv.at[col_part : col_part + col_all], {"sub": ahead})),
        (goes & has_down, comes & has_up, remote(3, col_send.at[col_all - col_part : col_all], col_recv.at[0:col_part], {"band": band + 1, "sub": ahead})),
        (goes & has_up, comes & has_down, remote(4, col_send.at[0:col_part], col_recv.at[col_part + col_all : 2 * col_part + col_all], {"band": band - 1, "sub": ahead})),
    ]
    for go, come, copy in sends[:2]:
        pl.when(go)(copy.start)
    cond_copy = remote(5, cond_ref, cond_recv, partner)
    cond_copy.start()

    bodies = [stand(lat_ref[:, y, :]) for y in range(height)]
    for y in range(0, height, 2):
        pair = [
            jnp.where(first_core, bodies[y + k][full_cols - side :], bodies[y + k][:side]) for k in range(2)
        ]
        col_send[y * side : (y + 2) * side, :] = jnp.concatenate(pair, axis=0).astype(jnp.bfloat16)

    for go, come, copy in sends[2:]:
        pl.when(go)(copy.start)

    mid_copy.wait()
    for i in range(3):
        for j in range(3):
            turned_mid = jnp.transpose(mid_ref[i, j])
            base = i * depth
            wide_ref[base + j * wide : base + (j + 1) * wide, :] = turned_mid[:wide, :wide]
            narrow_ref[j * wide : (j + 1) * wide, i * rest : (i + 1) * rest] = turned_mid[:wide, wide:]
            spot = 3 * wide + j * rest
            wide_ref[base + spot : base + spot + rest, :] = turned_mid[wide:, :wide]
            narrow_ref[spot : spot + rest, i * rest : (i + 1) * rest] = turned_mid[wide:, wide:]
            small = wout_ref[i, j].astype(jnp.float32)
            tall = jnp.transpose(jnp.concatenate([small] * copies, axis=0)).astype(jnp.bfloat16)
            span = slice(i * LANES // 2, (i + 1) * LANES // 2) if i < 2 else slice(LANES, 2 * LANES)
            tall = tall[:, : span.stop - span.start]
            last_ref[j * wide : (j + 1) * wide, span] = tall[:wide]
            last_ref[spot : spot + rest, span] = tall[wide:]
        spare = 3 * wide + 3 * rest
        wide_ref[i * depth + spare : (i + 1) * depth, :] = jnp.zeros((depth - spare, wide), jnp.bfloat16)
    narrow_ref[spare:, :] = jnp.zeros((depth - spare, 3 * rest), jnp.bfloat16)
    last_ref[spare:, :] = jnp.zeros((depth - spare, 2 * LANES), jnp.bfloat16)

    cond_copy.wait()
    time_copy.wait()
    plain = jnp.where(first_core, cond_ref[...], cond_recv[...])
    steered = jnp.where(first_core, cond_recv[...], cond_ref[...])
    half_rstd = 0.5 * rstd_ref[...]
    vec_ref[0:2, :] = half_rstd
    moments = lax.broadcasted_iota(jnp.int32, time_ref.shape, 1)
    for step in range(steps):
        column = jnp.sum(jnp.where(moments == time_at[step], time_ref[...], 0.0), axis=1, keepdims=True)
        time_row = jnp.transpose(jnp.broadcast_to(column, (feat, LANES)))[0:1]
        for layer in range(2):
            for q, cond in enumerate((plain, steered)):
                line = 2 + 4 * step + 2 * layer + q
                vec_ref[line : line + 1, :] = (time_row + cond - mean_ref[layer : layer + 1, :]) * half_rstd[layer : layer + 1, :]

    def wait_for(copy):
        def both():
            copy.wait_recv()

        return both

    for go, come, copy in sends:
        pl.when(go)(copy.wait_send)
        pl.when(come)(wait_for(copy))

    for row in range(rows):
        if margin <= row < margin + height:
            body = bodies[row - margin]
        else:
            spot = row if row < margin else row - height
            body = stand(row_recv[spot * chans : (spot + 1) * chans, :].astype(jnp.float32))
        pair = col_recv[row // 2 * 2 * side : (row // 2 * 2 + 2) * side, :].astype(jnp.float32)
        border = pair[row % 2 * side : (row % 2 + 1) * side]
        field = jnp.where(
            first_core,
            jnp.concatenate([border, body[: cols + side]], axis=0),
            jnp.concatenate([body[full_cols - cols - side :], border], axis=0),
        )
        state[row * stride : (row + 1) * stride, :] = jnp.where(inside(row - margin, LANES), field, 0.0)

    group = lax.broadcasted_iota(jnp.int32, (stride, LANES), 1) // chans

    def silu_of(half):
        return half + half * jnp.tanh(half)

    def spread(ref, row, big, small):
        for tap in range(3):
            ref[at(row), tap * wide : (tap + 1) * wide] = turned(big, tap).astype(jnp.bfloat16)
        ends = [turned(small, tap) for tap in range(3)]
        ends.append(jnp.zeros((stride, depth - 3 * wide - 3 * rest), jnp.float32))
        ref[at(row), 3 * wide : depth] = jnp.concatenate(ends, axis=1).astype(jnp.bfloat16)

    for step in range(steps):
        edge = margin - 3 * step
        now_rows = height + 2 * edge
        firsts = now_rows - 2
        seconds = now_rows - 4
        is_last = step == steps - 1
        base = 2 + 4 * step

        def lay(row, carry):
            field = state[at(row), :]
            before = turned(field, 0)
            after = turned(field, 2)
            mixed[at(row), 0:LANES] = jnp.where(group % 3 == 0, before, jnp.where(group % 3 == 1, field, after))
            mixed[at(row), LANES : 2 * LANES] = after
            return carry

        lax.fori_loop(0, now_rows, lay, 0, unroll=True)

        chunk = 6 if firsts % 6 == 0 else 2

        def lead(k, carry):
            row = k * chunk
            for m in range(chunk):
                one = mixed[at(row + m), 0:LANES]
                two = mixed[at(row + m + 1), 0:LANES]
                three = mixed[at(row + m + 2), 0:LANES]
                body = jnp.where(group < 3, one, jnp.where(group < 6, two, three))
                taps[at(row + m), 0:LANES] = body.astype(jnp.bfloat16)
                taps[at(row + m), LANES : LANES + chans] = mixed[at(row + m + 2), LANES : LANES + chans].astype(jnp.bfloat16)
            field = jnp.dot(taps[at(row, chunk), :], win_ref[...], preferred_element_type=jnp.float32)
            first[at(row, chunk), :] = field
            for q in range(2):
                shift = vec_ref[base + q : base + q + 1, :]
                for m in range(chunk):
                    here = field[m * stride : (m + 1) * stride]
                    keep = inside(row + m + 1 - edge, wide)
                    parts = []
                    for part in (slice(0, wide), slice(wide, feat)):
                        value = silu_of(here[:, part] * vec_ref[0:1, part] + shift[:, part])
                        parts.append(jnp.where(keep[:, : value.shape[1]], value, 0.0))
                    spread(lifts[q], row + m, *parts)
                thins[q][at(row, chunk), :] = jnp.dot(
                    lifts[q][at(row, chunk), :], narrow_ref[...], preferred_element_type=jnp.float32
                )
            return carry

        lax.fori_loop(0, firsts // chunk, lead, 0, unroll=True)

        count2 = 4 if seconds % 4 == 0 else (5 if seconds % 5 == 0 else 2)
        gain = table[2, coef_at[step]]

        def middle(k, carry):
            row = k * count2
            found = []
            for q in range(2):
                window = jnp.concatenate([lifts[q][at(row + tap, count2), :] for tap in range(3)], axis=1)
                total = first[at(row + 1, count2), 0:wide] + jnp.dot(
                    window, wide_ref[...], preferred_element_type=jnp.float32
                )
                tail = first[at(row + 1, count2), wide:feat]
                for tap in range(3):
                    tail = tail + thins[q][at(row + tap, count2), tap * rest : (tap + 1) * rest]
                shift = vec_ref[base + 2 + q : base + 3 + q, :]
                found.append(
                    [
                        silu_of(field * vec_ref[1:2, part] + shift[:, part])
                        for field, part in ((total, slice(0, wide)), (tail, slice(wide, feat)))
                    ]
                )
            lowered = [a + gain * (b - a) for a, b in zip(*found)]
            for m in range(count2):
                keep = inside(row + m + 2 - edge, wide)
                spread(
                    low,
                    row + m,
                    *[
                        jnp.where(keep[:, : part.shape[1]], part[m * stride : (m + 1) * stride], 0.0)
                        for part in lowered
                    ],
                )
            noise[at(row, count2), :] = jnp.dot(low[at(row, count2), :], last_ref[...], preferred_element_type=jnp.float32)
            return carry

        lax.fori_loop(0, seconds // count2, middle, 0, unroll=True)

        keeps = table[0, coef_at[step]]
        adds = table[1, coef_at[step]]

        def finish(row, carry):
            total = jnp.where(group < LANES // 2 // chans, noise[at(row), 0:LANES], noise[at(row + 1), 0:LANES])
            total = total + pltpu.roll(total, LANES // 2, 1) + noise[at(row + 2), LANES : 2 * LANES]
            value = keeps * state[at(row + 3), :] + adds * total
            if not is_last:
                value = jnp.where(inside(row + 3 - edge, LANES), value, 0.0)
            state[at(row), :] = value
            return carry

        lax.fori_loop(0, now_rows - 6, finish, 0, unroll=True)

    group = lax.broadcasted_iota(jnp.int32, (cols, LANES), 1) // chans
    packed = state[side : side + cols, :]
    for y in range(1, height):
        packed = jnp.where(group == y, state[y * stride + side : y * stride + side + cols, :], packed)
    half_send[...] = packed
    swap = remote(6, half_send, half_recv, partner)
    swap.start()
    swap.wait()
    other = half_recv[...]
    joined = jnp.concatenate(
        [jnp.where(first_core, packed, other), jnp.where(first_core, other, packed)], axis=0
    )
    flat = jnp.transpose(joined)
    for y in range(height):
        out_ref[y] = flat[y * chans : (y + 1) * chans]


def shards(
    latents, in_weight, mid_weight, out_weight, norm_mean, norm_rstd,
    cond_embed, time_embed, time_index, coef_index, sampler_table,
):
    chans, height, full_cols = latents.shape
    feat = in_weight.shape[3]
    steps = time_index.shape[0]
    margin = 3 * steps
    cols = full_cols // lax.axis_size("cfg")
    stride = up(cols + 2 * margin, 16)
    side = (stride - cols) // 2
    rows = height + 2 * margin
    wide = feat // TILE * TILE
    rest = feat - wide
    depth = 3 * wide + up(3 * rest, TILE)
    win = in_weight.reshape(9 * chans, feat)
    geom = (steps, height, full_cols, cols, stride, margin, feat, chans)
    whole = pl.BlockSpec(memory_space=pltpu.VMEM)
    scalars = pl.BlockSpec(memory_space=pltpu.SMEM)
    far = pl.BlockSpec(memory_space=pl.ANY)
    firsts = (rows - 2) * stride
    seconds = (rows - 4) * stride
    out = pl.pallas_call(
        functools.partial(section_kernel, geom),
        out_shape=jax.ShapeDtypeStruct((height, chans, full_cols), jnp.float32),
        in_specs=[scalars] * 3 + [whole, whole, far, whole, whole, whole, whole, far],
        out_specs=whole,
        scratch_shapes=[
            pltpu.VMEM((rows * stride, LANES), jnp.float32),
            pltpu.VMEM((firsts, 9 * chans), jnp.bfloat16),
            pltpu.VMEM((firsts, feat), jnp.float32),
            pltpu.VMEM((firsts, depth), jnp.bfloat16),
            pltpu.VMEM((firsts, depth), jnp.bfloat16),
            pltpu.VMEM((firsts, 3 * rest), jnp.float32),
            pltpu.VMEM((firsts, 3 * rest), jnp.float32),
            pltpu.VMEM((seconds, depth), jnp.bfloat16),
            pltpu.VMEM((rows * stride, 2 * LANES), jnp.float32),
            pltpu.VMEM((seconds, 2 * LANES), jnp.float32),
            pltpu.VMEM(mid_weight.shape, mid_weight.dtype),
            pltpu.VMEM(time_embed.shape[::-1], time_embed.dtype),
            pltpu.VMEM((3 * depth, wide), jnp.bfloat16),
            pltpu.VMEM((depth, 3 * rest), jnp.bfloat16),
            pltpu.VMEM((depth, 2 * LANES), jnp.bfloat16),
            pltpu.VMEM((up(2 + 4 * steps, 8), feat), jnp.float32),
            pltpu.VMEM((height * chans, full_cols), jnp.bfloat16),
            pltpu.VMEM((2 * margin * chans, full_cols), jnp.bfloat16),
            pltpu.VMEM((height * side, LANES), jnp.bfloat16),
            pltpu.VMEM((rows * side, LANES), jnp.bfloat16),
            pltpu.VMEM(cond_embed.shape, jnp.float32),
            pltpu.VMEM((cols, LANES), jnp.float32),
            pltpu.VMEM((cols, LANES), jnp.float32),
            pltpu.VMEM((stride, wide), jnp.int32),
            pltpu.SemaphoreType.DMA((2,)),
            pltpu.SemaphoreType.DMA((7,)),
            pltpu.SemaphoreType.DMA((7,)),
        ],
        compiler_params=pltpu.CompilerParams(
            vmem_limit_bytes=52 * 1024 * 1024, collective_id=0, has_side_effects=True
        ),
    )(
        time_index, coef_index, sampler_table, latents, win, mid_weight, out_weight,
        norm_mean, norm_rstd, cond_embed, time_embed.T,
    )
    return jnp.transpose(out, (1, 0, 2))


def solution(mesh):
    return jax.shard_map(
        shards,
        mesh=mesh,
        in_specs=(P("groups", "band", "sub"), P(), P(), P(), P(), P(), P("cfg", "groups"), P(), P(), P(), P()),
        out_specs=P("groups", "band", "sub"),
        check_vma=False,
    )
```
